128 devices in a mesh: seq: 16 (over x, y), db: 8 (over z, core).
Axes of the slice: x: 4, y: 4, z: 4, core: 2. Of those that a mesh axis runs over, the one named last changes fastest.
Arguments:
- decoder: bfloat16 [16384, 4096], P('seq'), may hold values from -6 to 6
- w_query: bfloat16 [4096, 4096], P(None, 'db'), may hold values from -0.09375 to 0.09375
- w_key: bfloat16 [896, 4096], P(None, 'db'), may hold values from -0.1875 to 0.1875
- w_value: bfloat16 [896, 4096], P(None, 'db'), may hold values from -0.1875 to 0.1875
- w_out: bfloat16 [4096, 4096], P('db'), may hold values from -0.09375 to 0.09375
- database: bfloat16 [384, 128, 896], P('seq'), may hold values from -240 to 240
- nb_shard: int32 [256, 2], replicated, may hold values from 0 to 15, as said below
- nb_slot: int32 [256, 2], replicated, may hold values from 0 to 23
Outputs:
- attended: bfloat16 [16384, 4096], P(('seq', 'db'))
The draws below stay inside these ranges and needn't reach their ends.
Inputs may be any that keep to these rules, and one draw needn't show every extreme that they name: `nb_shard`: the 32 entries of each 16 consecutive spans name any one shard at most 3 times, and one shard exactly 3 times.
All inputs are finite; a program needn't handle non-finite values.
Results may differ from the reference program's by a relative error of at most 0.022.
The reference program's roundings to bfloat16 on the way (of `normed`, `queries`, `keys`, `values`, `probs` and `context`) count: a program that leaves them out, or rounds other values in their place, can miss the bound.
Values may be sent and summed in bfloat16 or wider, within the bound.
No kernel may reach another device: no remote copies, remote signals or barrier semaphores. Data moves between devices by JAX's collectives and lax.ppermute only.
A program may use at most 128 MiB of HBM per device.

```python
import math
import jax
import jax.numpy as jnp
from jax import lax

D = 4096
HEADS = 32
HS = 128
EW = 896
CL = 64
NB_LEN = 128
NEIGH = 2
CH_SEQ = 16
SLOTS = 24
TOKENS = 16384
SPANS = 256
SHARDS = 16
NREQ = 32
CAP = 3
N_SEQ = 16
N_DB = 8


def draw_nb_shard(key, part):
    key = jax.random.fold_in(key, 7)

    def one_group(group_key):
        key_hot, key_rest, key_order = jax.random.split(group_key, 3)
        hottest = jax.random.randint(key_hot, (), 0, SHARDS).astype(jnp.int32)
        places = jax.random.permutation(key_rest, (SHARDS - 1) * CAP)[:NREQ - CAP]
        others = (places // CAP).astype(jnp.int32)
        others = others + (others >= hottest).astype(jnp.int32)
        listed = jnp.concatenate([jnp.full((CAP,), hottest, jnp.int32), others])
        return jax.random.permutation(key_order, listed)
    groups = jax.vmap(one_group)(jax.random.split(key, SHARDS))
    return groups.reshape(SPANS, NEIGH).astype(jnp.int32)


def draw_database(key, part):
    key = jax.random.fold_in(key, 19)
    key_base = jax.random.fold_in(key, 0)
    base = jnp.clip(jax.random.normal(key_base, (SHARDS * SLOTS, NB_LEN, EW), jnp.float32), -6.0, 6.0)
    return base.astype(jnp.bfloat16)


def plant(array, stream_key, smallest, top_value):
    longest = array.shape.index(max(array.shape))
    spots = []
    for shift in (0, 1):
        where = [jax.random.randint(jax.random.fold_in(stream_key, axis), (), 0, length) for axis, length in enumerate(array.shape)]
        where[longest] = (where[longest] + shift) % array.shape[longest]
        spots.append(tuple(where))
    return array.at[spots[0]].set(smallest).at[spots[1]].set(top_value)


def steps_of(own_key, shape, cuts, smallest, high):
    def one(axis_at, blocks):
        steps = jax.random.uniform(jax.random.fold_in(jax.random.fold_in(own_key, 6), axis_at), (blocks,), jnp.float32, smallest / len(cuts), high / len(cuts))
        return jnp.repeat(jnp.exp(steps), shape[axis_at] // blocks).reshape((-1,) + (1,) * (len(shape) - axis_at - 1))

    level = one(*cuts[0])
    for cut in cuts[1:]:
        level = level * one(*cut)
    return level


def bell_draw(key, extent, scale, bound, cuts=(), held_as=jnp.bfloat16):
    gain = steps_of(key, extent, cuts, -0.22, 0.18) if cuts else 1.0
    array = jax.random.normal(key, extent, jnp.float32) * scale * gain
    return jnp.minimum(jnp.maximum(array, -bound), bound).astype(held_as)


def setup_inputs(seed: int = 0) -> dict:
    key_of = jax.random.split(jax.random.key(seed), 9)
    decoder = bell_draw(key_of[0], (TOKENS, D), 1.0, 6.0, ((0, 16),))
    w_query = bell_draw(key_of[1], (D, HEADS * HS), D ** -0.5, 0.09375, ((1, 8),))
    w_key = bell_draw(key_of[2], (EW, HEADS * HS), EW ** -0.5, 0.1875, ((1, 8),))
    w_value = bell_draw(key_of[3], (EW, HEADS * HS), EW ** -0.5, 0.1875, ((1, 8),))
    w_out = bell_draw(key_of[4], (HEADS * HS, D), (HEADS * HS) ** -0.5, 0.09375, ((0, 8),))
    database = draw_database(jax.random.fold_in(key_of[8], 71), 0)
    nb_shard = draw_nb_shard(jax.random.fold_in(key_of[8], 71), 0)
    nb_slot = plant(jax.random.randint(key_of[7], (SPANS, NEIGH), 0, SLOTS), jax.random.fold_in(key_of[7], 1), 0, SLOTS - 1).astype(jnp.int32)
    return dict(decoder=decoder, w_query=w_query, w_key=w_key, w_value=w_value, w_out=w_out, database=database, nb_shard=nb_shard, nb_slot=nb_slot)


def attend(queries, keys, values):
    blocks, qlen, width = queries.shape
    heads_here = width // HS
    q_heads = queries.astype(jnp.float32).reshape(blocks, qlen, heads_here, HS)
    k_heads = keys.astype(jnp.float32).reshape(blocks, keys.shape[1], heads_here, HS)
    v_heads = values.astype(jnp.float32).reshape(blocks, values.shape[1], heads_here, HS)
    scores = jnp.einsum('bqhd,bkhd->bhqk', q_heads, k_heads) * (1.0 / math.sqrt(HS))
    probs = jax.nn.softmax(scores, axis=-1).astype(jnp.bfloat16)
    context = jnp.einsum('bhqk,bkhd->bqhd', probs.astype(jnp.float32), v_heads)
    return context.reshape(blocks, qlen, width).astype(jnp.bfloat16)

def reference(decoder, w_query, w_key, w_value, w_out, database, nb_shard, nb_slot):
    source = decoder.astype(jnp.float32)
    scale = lax.rsqrt(lax.optimization_barrier(jnp.mean(source * source, axis=-1, keepdims=True)) + 1e-05)
    normed = (source * scale).astype(jnp.bfloat16)
    queries = jnp.dot(normed, w_query, preferred_element_type=jnp.float32).astype(jnp.bfloat16)
    width = queries.shape[1]
    shifted = jnp.concatenate([queries[CL - 1:], jnp.zeros((CL - 1, width), jnp.bfloat16)], axis=0)
    shifted = shifted.reshape(N_SEQ, CH_SEQ, CL, width)
    flat_index = (nb_shard * SLOTS + nb_slot).astype(jnp.int32).reshape(N_SEQ, CH_SEQ * NEIGH)
    key_weight = w_key.astype(jnp.float32)
    value_weight = w_value.astype(jnp.float32)

    def one_block(inputs):
        block_queries, block_index = inputs
        rows = database[block_index].reshape(CH_SEQ, NEIGH * NB_LEN, EW).astype(jnp.float32)
        keys = jnp.einsum('cne,eh->cnh', rows, key_weight).astype(jnp.bfloat16)
        values = jnp.einsum('cne,eh->cnh', rows, value_weight).astype(jnp.bfloat16)
        return attend(block_queries, keys, values)
    aligned = lax.map(one_block, (shifted, flat_index)).reshape(TOKENS, width)
    context = jnp.concatenate([jnp.zeros((CL - 1, width), jnp.bfloat16), aligned[:TOKENS - CL + 1]], axis=0)
    group_width = width // N_DB
    total = jnp.zeros((TOKENS, D), jnp.float32)
    for head_group in range(N_DB):
        lower = head_group * group_width
        partial_sum = jnp.dot(context[:, lower:lower + group_width], w_out[lower:lower + group_width], preferred_element_type=jnp.float32).astype(jnp.bfloat16)
        total = total + lax.optimization_barrier(partial_sum).astype(jnp.float32)
    return total.astype(jnp.bfloat16)
```

```python
import math

import jax
import jax.numpy as jnp
from jax import lax
from jax.experimental import pallas as pl
from jax.experimental.pallas import tpu as pltpu
from jax.sharding import Mesh, PartitionSpec as P

HS = 128
CL = 64
NB_LEN = 128
NEIGH = 2
N_Z = 4
N_CORE = 2
BLOCK = 128
HALO = CL - 1
KEPT = BLOCK - HALO
F32 = jnp.float32
BF16 = jnp.bfloat16


def step(value, axis, steps):
    count = lax.axis_size(axis)
    return lax.ppermute(value, axis, [(i, (i + steps) % count) for i in range(count)])


def dot(a, b):
    return jnp.dot(a, b, preferred_element_type=F32)


def bucket_places(shards):
    count = shards.shape[1]
    same_shard = shards[:, :, None] == shards[:, None, :]
    earlier = jnp.arange(count)[None, :] < jnp.arange(count)[:, None]
    return jnp.sum((same_shard & earlier[None]).astype(jnp.int32), axis=2)


def attend_kernel(qa_ref, qb_ref, *refs):
    parts_a, parts_b, out_ref = refs[0:4], refs[4:8], refs[8]
    half = qa_ref.shape[1]
    for side, (q_ref, parts) in enumerate(((qa_ref, parts_a), (qb_ref, parts_b))):
        for head in range(half // HS):
            lower = head * HS
            q = q_ref[:, lower : lower + HS]
            k = jnp.concatenate([part[0, :, lower : lower + HS] for part in parts], axis=0)
            v = jnp.concatenate([part[0, :, half + lower : half + lower + HS] for part in parts], axis=0)
            scores = lax.dot_general(q, k, (((1,), (1,)), ((), ())), preferred_element_type=F32)
            scores = scores * (1.0 / math.sqrt(HS))
            top = jnp.max(scores, axis=-1, keepdims=True)
            weights = jnp.exp(scores - top)
            total = jnp.sum(weights, axis=-1, keepdims=True)
            probs = (weights * (1.0 / total)).astype(BF16)
            out_ref[:, side * half + lower : side * half + lower + HS] = dot(probs, v).astype(BF16)


def attend(queries_a, queries_b, parts_a, parts_b):
    tokens, half = queries_a.shape
    spans = tokens // CL
    q_spec = pl.BlockSpec((CL, half), lambda i: (i, 0))
    part_spec = pl.BlockSpec((1,) + parts_a[0].shape[1:], lambda i: (i, 0, 0))
    return pl.pallas_call(
        attend_kernel,
        grid=(spans,),
        in_specs=[q_spec, q_spec] + [part_spec] * 8,
        out_specs=pl.BlockSpec((CL, 2 * half), lambda i: (i, 0)),
        out_shape=jax.ShapeDtypeStruct((tokens, 2 * half), BF16),
        cost_estimate=pl.CostEstimate(
            flops=4 * tokens * 256 * 2 * half, bytes_accessed=tokens * 40 * half, transcendentals=tokens * 2048
        ),
        compiler_params=pltpu.CompilerParams(vmem_limit_bytes=32 * 1024 * 1024),
    )(queries_a, queries_b, *parts_a, *parts_b)


def body(decoder, w_query, w_key, w_value, w_out, database, nb_shard, nb_slot):
    n_seq = lax.axis_size("seq")
    seq_index, z_index, core = lax.axis_index("seq"), lax.axis_index("z"), lax.axis_index("core")
    tok_rows, model = decoder.shape
    half = w_query.shape[1]
    requests = NEIGH * (tok_rows // CL)
    capacity = (requests + n_seq - 1) // n_seq + 1
    enc = database.shape[2]
    piece = NB_LEN // (N_Z * N_CORE)

    halo = lax.ppermute(decoder[:CL], "seq", [(i + 1, i) for i in range(n_seq - 1)])

    shard_lists = nb_shard.reshape(n_seq, requests)
    slot_lists = nb_slot.reshape(n_seq, requests)
    places = bucket_places(shard_lists)
    picked = (shard_lists == seq_index)[:, None, :] & (places[:, None, :] == jnp.arange(capacity)[None, :, None])
    send_slot = jnp.sum(jnp.where(picked, slot_lists[:, None, :], 0), axis=2)
    my_piece = lax.dynamic_slice_in_dim(database, (z_index * N_CORE + core) * piece, piece, axis=1)
    received = lax.all_to_all(my_piece[send_slot], "seq", split_axis=0, concat_axis=0, tiled=True)
    received = received.reshape(n_seq * capacity, piece, enc)
    my_shards = lax.dynamic_index_in_dim(shard_lists, seq_index, 0, keepdims=False)
    my_places = lax.dynamic_index_in_dim(places, seq_index, 0, keepdims=False)
    row_index = (my_shards * capacity + my_places).reshape(N_Z, N_CORE, -1)
    mine = lax.dynamic_index_in_dim(row_index, core, 1, keepdims=False).reshape(-1)
    theirs = lax.dynamic_index_in_dim(row_index, 1 - core, 1, keepdims=False).reshape(-1)
    swapped = step(received[theirs], "core", 1)
    own = jnp.concatenate([received[mine], swapped], axis=1)
    spans = requests // NEIGH // N_CORE
    own = own.reshape(spans, NEIGH * 2 * piece, enc)
    low, high = own[: spans // 2], own[spans // 2 :]

    w_kv = jnp.concatenate([w_key, w_value], axis=1)
    w_kv_other = step(w_kv, "core", 1)
    w_query_other = step(w_query, "core", 1)
    w_out_other = step(w_out, "core", 1)
    w_out_chip = jnp.concatenate([w_out, w_out_other], axis=0)

    tokens = jnp.concatenate([decoder[CL - 1 :], halo[: CL - 1]], axis=0).reshape(N_Z, N_CORE, BLOCK, model)
    tokens = lax.dynamic_index_in_dim(tokens, core, 1, keepdims=False).reshape(N_Z * BLOCK, model)
    source = tokens.astype(F32)
    scale = lax.rsqrt(jnp.mean(source * source, axis=-1, keepdims=True) + 1e-05)
    normed = (source * scale).astype(BF16)
    queries_a = dot(normed, w_query).astype(BF16)
    queries_b = dot(normed, w_query_other).astype(BF16)

    up_low = step(low, "z", 1)
    down_high = step(high, "z", -1)
    up_high = step(high, "z", 1)
    down_low = step(low, "z", -1)
    far_low = step(up_low, "z", 1)
    far_high = step(down_high, "z", -1)

    def project(rows, weight):
        flat = rows.reshape(-1, enc)
        return dot(flat, weight).astype(BF16).reshape(rows.shape[0], rows.shape[1], -1)

    contexts = []
    for place, parts in enumerate(((low, up_low, down_low, far_low), (high, up_high, down_high, far_high))):
        lower = place * N_Z * BLOCK // 2
        contexts.append(
            attend(
                queries_a[lower : lower + N_Z * BLOCK // 2],
                queries_b[lower : lower + N_Z * BLOCK // 2],
                [project(part, w_kv) for part in parts],
                [project(part, w_kv_other) for part in parts],
            )
        )
    context = jnp.concatenate(contexts, axis=0).reshape(N_Z, BLOCK, 2 * half)

    tails = context[:, KEPT:]
    tails = jnp.concatenate([tails[:, :, half:], tails[:, :, :half]], axis=2)
    heads = step(tails, "core", 1)
    first = lax.ppermute(tails[N_Z - 1], ("seq", "core"), [(2 * i + 1, 2 * i + 2) for i in range(n_seq - 1)])
    heads = jnp.where(core == 0, jnp.concatenate([first[None], heads[:-1]], axis=0), heads)
    context = jnp.concatenate([heads, context[:, :KEPT]], axis=1)

    def block(distance):
        return lax.dynamic_index_in_dim(context, (z_index + distance) % N_Z, 0, keepdims=False)

    side = model // 2
    w_left, w_right = w_out_chip[:, :side], w_out_chip[:, side:]
    far = block(2)
    up_far = step(dot(far, w_left).astype(BF16), "z", 1)
    down_far = step(dot(far, w_right).astype(BF16), "z", -1)
    above, below, here = block(1), block(3), block(0)
    up_right = step(dot(above, w_right).astype(BF16), "z", 1)
    down_left = step(dot(below, w_left).astype(BF16), "z", -1)
    up_left = step((dot(above, w_left) + up_far.astype(F32)).astype(BF16), "z", 1)
    down_right = step((dot(below, w_right) + down_far.astype(F32)).astype(BF16), "z", -1)
    left = dot(here, w_left) + down_left.astype(F32) + up_left.astype(F32)
    right = dot(here, w_right) + up_right.astype(F32) + down_right.astype(F32)
    return jnp.concatenate([left.astype(BF16), right.astype(BF16)], axis=1)


def solution(mesh):
    n_seq = mesh.devices.shape[0]
    fine = Mesh(mesh.devices.reshape(n_seq, N_Z, N_CORE), ("seq", "z", "core"))
    db = ("z", "core")
    return jax.shard_map(
        body,
        mesh=fine,
        in_specs=(
            P("seq", None),
            P(None, db),
            P(None, db),
            P(None, db),
            P(db, None),
            P("seq", None, None),
            P(),
            P(),
        ),
        out_specs=P(("seq", "z", "core"), None),
        check_vma=False,
    )
```

```python
import math

import jax
import jax.numpy as jnp
from jax import lax
from jax.experimental import pallas as pl
from jax.experimental.pallas import tpu as pltpu
from jax.sharding import Mesh, PartitionSpec as P

HS = 128
CL = 64
NB_LEN = 128
NEIGH = 2
N_Z = 4
N_CORE = 2
BLOCK = 128
F32 = jnp.float32
BF16 = jnp.bfloat16


def step(value, axis, steps):
    count = lax.axis_size(axis)
    return lax.ppermute(value, axis, [(i, (i + steps) % count) for i in range(count)])


def dot(a, b):
    return jnp.dot(a, b, preferred_element_type=F32)


def bucket_places(shards):
    count = shards.shape[1]
    same_shard = shards[:, :, None] == shards[:, None, :]
    earlier = jnp.arange(count)[None, :] < jnp.arange(count)[:, None]
    return jnp.sum((same_shard & earlier[None]).astype(jnp.int32), axis=2)


def attend_kernel(q_ref, *refs):
    parts_a, parts_b, out_ref = refs[0:4], refs[4:8], refs[8]
    half = q_ref.shape[1] // 2
    scores = []
    for side, parts in enumerate((parts_a, parts_b)):
        for lower in range(0, half, HS):
            q = q_ref[:, side * half + lower : side * half + lower + HS]
            k = jnp.concatenate([part[:, lower : lower + HS] for part in parts], axis=0)
            scores.append(lax.dot_general(q, k, (((1,), (1,)), ((), ())), preferred_element_type=F32))
    probs = []
    for score in scores:
        score = score * (1.0 / math.sqrt(HS))
        weights = jnp.exp(score - jnp.max(score, axis=-1, keepdims=True))
        total = jnp.sum(weights, axis=-1, keepdims=True)
        probs.append((weights * (1.0 / total)).astype(BF16))
    for side, parts in enumerate((parts_a, parts_b)):
        for lower in range(0, half, HS):
            v = jnp.concatenate([part[:, half + lower : half + lower + HS] for part in parts], axis=0)
            out_ref[:, side * half + lower : side * half + lower + HS] = dot(
                probs[(side * half + lower) // HS], v
            ).astype(BF16)


def attend(queries, parts_a, parts_b, parity):
    tokens, width = queries.shape
    spans = tokens // CL
    q_spec = pl.BlockSpec((CL, width), lambda i: (i, 0))
    part_spec = pl.BlockSpec((parts_a[0].shape[0] // (2 * spans), width), lambda i: (2 * i + parity, 0))
    return pl.pallas_call(
        attend_kernel,
        grid=(spans,),
        in_specs=[q_spec] + [part_spec] * 8,
        out_specs=q_spec,
        out_shape=jax.ShapeDtypeStruct((tokens, width), BF16),
        cost_estimate=pl.CostEstimate(
            flops=4 * tokens * 256 * width, bytes_accessed=tokens * 20 * width, transcendentals=tokens * 2048
        ),
        compiler_params=pltpu.CompilerParams(vmem_limit_bytes=32 * 1024 * 1024),
    )(queries, *parts_a, *parts_b)


def project_kernel(low_ref, high_ref, wa_ref, wb_ref, out_a_ref, out_b_ref):
    rows = jnp.concatenate([low_ref[...], high_ref[...]], axis=0)
    out_a_ref[...] = dot(rows, wa_ref[...]).astype(BF16)
    out_b_ref[...] = dot(rows, wb_ref[...]).astype(BF16)


def project(low, high, weight_a, weight_b):
    rows, enc = low.shape
    width = weight_a.shape[1]
    tile = width // 2
    row_spec = pl.BlockSpec((rows, enc), lambda i: (0, 0))
    weight_spec = pl.BlockSpec((enc, tile), lambda i: (0, i))
    out_spec = pl.BlockSpec((2 * rows, tile), lambda i: (0, i))
    out = jax.ShapeDtypeStruct((2 * rows, width), BF16)
    return pl.pallas_call(
        project_kernel,
        grid=(width // tile,),
        in_specs=[row_spec, row_spec, weight_spec, weight_spec],
        out_specs=[out_spec, out_spec],
        out_shape=[out, out],
        cost_estimate=pl.CostEstimate(
            flops=8 * rows * enc * width, bytes_accessed=4 * (rows + width) * enc + 8 * rows * width, transcendentals=0
        ),
        compiler_params=pltpu.CompilerParams(vmem_limit_bytes=32 * 1024 * 1024),
    )(low, high, weight_a, weight_b)


def swap_halves(value):
    half = value.shape[-1] // 2
    return jnp.concatenate([value[..., half:], value[..., :half]], axis=-1)


def body(decoder, w_query, w_key, w_value, w_out, database, nb_shard, nb_slot):
    n_seq = lax.axis_size("seq")
    seq_index, z_index, core = lax.axis_index("seq"), lax.axis_index("z"), lax.axis_index("core")
    tok_rows, model = decoder.shape
    half = w_query.shape[1]
    requests = NEIGH * (tok_rows // CL)
    capacity = (requests + n_seq - 1) // n_seq + 1
    enc = database.shape[2]
    piece = NB_LEN // (N_Z * N_CORE)

    shard_lists = nb_shard.reshape(n_seq, requests)
    slot_lists = nb_slot.reshape(n_seq, requests)
    places = bucket_places(shard_lists)
    picked = (shard_lists == seq_index)[:, None, :] & (places[:, None, :] == jnp.arange(capacity)[None, :, None])
    send_slot = jnp.sum(jnp.where(picked, slot_lists[:, None, :], 0), axis=2)
    my_piece = lax.dynamic_slice_in_dim(database, (z_index * N_CORE + core) * piece, piece, axis=1)
    received = lax.all_to_all(my_piece[send_slot], "seq", split_axis=0, concat_axis=0, tiled=True)
    received = received.reshape(n_seq * capacity, piece, enc)
    my_shards = lax.dynamic_index_in_dim(shard_lists, seq_index, 0, keepdims=False)
    my_places = lax.dynamic_index_in_dim(places, seq_index, 0, keepdims=False)
    row_index = (my_shards * capacity + my_places).reshape(N_Z, N_CORE, -1)
    mine = lax.dynamic_index_in_dim(row_index, core, 1, keepdims=False).reshape(-1)
    theirs = lax.dynamic_index_in_dim(row_index, 1 - core, 1, keepdims=False).reshape(-1)
    swapped = step(received[theirs], "core", 1)
    own = jnp.concatenate([received[mine], swapped], axis=1)
    spans = requests // NEIGH // N_CORE
    own = own.reshape(spans * NEIGH * 2 * piece, enc)
    low, high = own[: own.shape[0] // 2], own[own.shape[0] // 2 :]

    w_kv = jnp.concatenate([w_key, w_value], axis=1)
    w_query_other = step(w_query, "core", 1)
    w_kv_other = step(w_kv, "core", 1)
    w_out_other = step(w_out, "core", 1)
    w_out_chip = jnp.concatenate([w_out, w_out_other], axis=0)

    tokens = decoder.reshape(N_Z, N_CORE, BLOCK, model)
    tokens = lax.dynamic_index_in_dim(tokens, core, 1, keepdims=False).reshape(N_Z * BLOCK, model)
    source = tokens.astype(F32)
    scale = lax.rsqrt(jnp.mean(source * source, axis=-1, keepdims=True) + 1e-05)
    normed = (source * scale).astype(BF16)
    queries = jnp.concatenate([dot(normed, w_query).astype(BF16), dot(normed, w_query_other).astype(BF16)], axis=1)
    queries = jnp.roll(queries.reshape(N_Z, BLOCK, 2 * half), 1, axis=1)
    ahead, first_queries = queries[:, :CL], queries[:, CL:]
    is_first_row = lax.broadcasted_iota(jnp.int32, (1, CL, 1), 1) == 0
    leaving = swap_halves(ahead)
    arrived = step(leaving, "core", 1)
    crossing = lax.ppermute(leaving[0], ("seq", "core"), [(2 * i + 2, 2 * i + 1) for i in range(n_seq - 1)])
    arrived = jnp.where(core == 0, arrived, jnp.concatenate([arrived[1:], crossing[None]], axis=0))
    second_queries = jnp.where(is_first_row, ahead, arrived)

    up_low = step(low, "z", 1)
    down_high = step(high, "z", -1)
    up_high = step(high, "z", 1)
    down_low = step(low, "z", -1)
    far_low = step(up_low, "z", 1)
    far_high = step(down_high, "z", -1)
    pairs = [
        project(part_low, part_high, w_kv, w_kv_other)
        for part_low, part_high in ((low, high), (up_low, up_high), (down_low, down_high), (far_low, far_high))
    ]
    parts_a, parts_b = [pair[0] for pair in pairs], [pair[1] for pair in pairs]

    second = attend(second_queries.reshape(N_Z * CL, 2 * half), parts_a, parts_b, 1)
    second = second.reshape(N_Z, CL, 2 * half)
    leaving = swap_halves(second)
    arrived = step(leaving, "core", 1)
    crossing = lax.ppermute(leaving[N_Z - 1], ("seq", "core"), [(2 * i + 1, 2 * i + 2) for i in range(n_seq - 1)])
    arrived = jnp.where(core == 0, jnp.concatenate([crossing[None], arrived[:-1]], axis=0), arrived)
    first = attend(first_queries.reshape(N_Z * CL, 2 * half), parts_a, parts_b, 0)
    first = first.reshape(N_Z, CL, 2 * half)
    context = jnp.concatenate([jnp.where(is_first_row, second, arrived), first], axis=1)

    def block(distance):
        return lax.dynamic_index_in_dim(context, (z_index + distance) % N_Z, 0, keepdims=False)

    side = model // 2
    w_left, w_right = w_out_chip[:, :side], w_out_chip[:, side:]
    far = block(2)
    up_far = step(dot(far, w_left).astype(BF16), "z", 1)
    down_far = step(dot(far, w_right).astype(BF16), "z", -1)
    above, below, here = block(1), block(3), block(0)
    up_right = step(dot(above, w_right).astype(BF16), "z", 1)
    down_left = step(dot(below, w_left).astype(BF16), "z", -1)
    up_left = step((dot(above, w_left) + up_far.astype(F32)).astype(BF16), "z", 1)
    down_right = step((dot(below, w_right) + down_far.astype(F32)).astype(BF16), "z", -1)
    left = dot(here, w_left) + down_left.astype(F32) + up_left.astype(F32)
    right = dot(here, w_right) + up_right.astype(F32) + down_right.astype(F32)
    return jnp.roll(jnp.concatenate([left.astype(BF16), right.astype(BF16)], axis=1), -1, axis=0)


def solution(mesh):
    n_seq = mesh.devices.shape[0]
    fine = Mesh(mesh.devices.reshape(n_seq, N_Z, N_CORE), ("seq", "z", "core"))
    db = ("z", "core")
    return jax.shard_map(
        body,
        mesh=fine,
        in_specs=(
            P("seq", None),
            P(None, db),
            P(None, db),
            P(None, db),
            P(db, None),
            P("seq", None, None),
            P(),
            P(),
        ),
        out_specs=P(("seq", "z", "core"), None),
        check_vma=False,
    )
```

```python
import math

import jax
import jax.numpy as jnp
from jax import lax
from jax.experimental import pallas as pl
from jax.experimental.pallas import tpu as pltpu
from jax.sharding import Mesh, PartitionSpec as P

HS = 128
CL = 64
NB_LEN = 128
NEIGH = 2
N_Z = 4
N_CORE = 2
BLOCK = 128
F32 = jnp.float32
BF16 = jnp.bfloat16
SHARE = 0.4
LIMIT = 60 * 1024 * 1024


def step(value, axis, steps):
    count = lax.axis_size(axis)
    return lax.ppermute(value, axis, [(i, (i + steps) % count) for i in range(count)])


def cost(flops):
    return pl.CostEstimate(flops=int(flops * SHARE), bytes_accessed=int(flops * SHARE / 1000), transcendentals=0)


def dot(a, b):
    return jnp.dot(a, b, preferred_element_type=F32)


def bucket_places(shards):
    count = shards.shape[1]
    same_shard = shards[:, :, None] == shards[:, None, :]
    earlier = jnp.arange(count)[None, :] < jnp.arange(count)[:, None]
    return jnp.sum((same_shard & earlier[None]).astype(jnp.int32), axis=2)


def pick_kernel(index_ref, start_ref, source_ref, *refs):
    out_refs, rows_ref, sem = refs[:-2], refs[-2], refs[-1]
    rows = rows_ref.shape[1]
    start = pl.multiple_of(start_ref[0] * rows, rows)
    copy = pltpu.make_async_copy(source_ref.at[:, pl.ds(start, rows)], rows_ref, sem)
    copy.start()
    copy.wait()
    place = 0
    for out_ref in out_refs:
        for i in range(out_ref.shape[0]):
            out_ref[i] = rows_ref[index_ref[place]]
            place += 1


def pick(source, index, start, rows, counts):
    shapes = [(count, rows, source.shape[2]) for count in counts]
    return pl.pallas_call(
        pick_kernel,
        grid_spec=pltpu.PrefetchScalarGridSpec(
            num_scalar_prefetch=2,
            grid=(1,),
            in_specs=[pl.BlockSpec(memory_space=pltpu.HBM)],
            out_specs=[pl.BlockSpec(shape, lambda i, index, start: (0, 0, 0)) for shape in shapes],
            scratch_shapes=[pltpu.VMEM((source.shape[0], rows, source.shape[2]), source.dtype), pltpu.SemaphoreType.DMA],
        ),
        out_shape=[jax.ShapeDtypeStruct(shape, source.dtype) for shape in shapes],
        cost_estimate=cost(1e9),
        compiler_params=pltpu.CompilerParams(vmem_limit_bytes=LIMIT),
    )(index, start.reshape(1), source)


def query_kernel(core_ref, x_hbm, wa_hbm, wb_hbm, first_ref, second_ref, crossing_ref, x_ref, wa_ref, wb_ref, sems):
    half = wa_ref.shape[1]
    copies = []
    for j in range(N_Z):
        block = N_CORE * j + core_ref[0]
        after = lax.rem(block + 1, N_Z * N_CORE)
        copies.append(pltpu.make_async_copy(x_hbm.at[block], x_ref.at[j, :BLOCK], sems.at[2 * j]))
        copies.append(pltpu.make_async_copy(x_hbm.at[after, :CL], x_ref.at[j, BLOCK:], sems.at[2 * j + 1]))
    copies.append(pltpu.make_async_copy(wa_hbm, wa_ref, sems.at[2 * N_Z]))
    copies.append(pltpu.make_async_copy(wb_hbm, wb_ref, sems.at[2 * N_Z + 1]))
    for copy in copies:
        copy.start()
    for j in range(N_Z):
        copies[2 * j].wait()
        copies[2 * j + 1].wait()
        source = x_ref[j].astype(F32)
        scale = lax.rsqrt(jnp.mean(source * source, axis=-1, keepdims=True) + 1e-05)
        x_ref[j] = (source * scale).astype(BF16)
    rows = BLOCK + CL
    for i, weight_ref in enumerate((wa_ref, wb_ref)):
        copies[2 * N_Z + i].wait()
        here, there = slice(i * half, (i + 1) * half), slice((1 - i) * half, (2 - i) * half)
        product = dot(x_ref[...].reshape(N_Z * rows, -1), weight_ref[...])
        for j in range(N_Z):
            rolled = pltpu.roll(product[j * rows : (j + 1) * rows], 1, 0).astype(BF16)
            first_ref[j, :, here] = rolled[CL:BLOCK]
            second_ref[j, :, here] = rolled[BLOCK:]
            if j == 0:
                crossing_ref[:, there] = rolled[:CL]


def project_queries(decoder, weight_a, weight_b, core):
    model, half = weight_a.shape
    blocks = decoder.reshape(N_Z * N_CORE, BLOCK, model)
    shape = (N_Z, CL, 2 * half)
    out_spec = pl.BlockSpec(shape, lambda i, core: (0, 0, 0))
    return pl.pallas_call(
        query_kernel,
        grid_spec=pltpu.PrefetchScalarGridSpec(
            num_scalar_prefetch=1,
            grid=(1,),
            in_specs=[pl.BlockSpec(memory_space=pltpu.HBM)] * 3,
            out_specs=[out_spec, out_spec, pl.BlockSpec(shape[1:], lambda i, core: (0, 0))],
            scratch_shapes=[
                pltpu.VMEM((N_Z, BLOCK + CL, model), BF16),
                pltpu.VMEM((model, half), BF16),
                pltpu.VMEM((model, half), BF16),
                pltpu.SemaphoreType.DMA((2 * N_Z + 2,)),
            ],
        ),
        out_shape=[jax.ShapeDtypeStruct(dims, BF16) for dims in (shape, shape, shape[1:])],
        cost_estimate=cost(3e9),
        compiler_params=pltpu.CompilerParams(vmem_limit_bytes=LIMIT),
    )(core.reshape(1), blocks, weight_a, weight_b)


def span_kernel(place_ref, q_hbm, crossing_hbm, *refs):
    row_hbm, weight_hbm, out_hbm, out_refs = refs[:8], refs[8:14], refs[14:22], refs[22:30]
    q_ref, crossing_ref, rows_ref, weight_refs, kv_ref, context_ref, sems, out_sem = (
        *refs[30:33],
        refs[33:39],
        *refs[39:43],
    )
    half, model = weight_refs[4].shape
    parts, rows, enc = rows_ref.shape
    row_copies = [pltpu.make_async_copy(row_hbm[i], rows_ref.at[i], sems.at[i]) for i in range(parts)]
    weight_copies = [pltpu.make_async_copy(weight_hbm[i], weight_refs[i], sems.at[8 + i]) for i in range(6)]
    query_copies = [
        pltpu.make_async_copy(q_hbm, q_ref, sems.at[14]),
        pltpu.make_async_copy(crossing_hbm, crossing_ref, sems.at[15]),
    ]
    for copy in row_copies + weight_copies[:4] + query_copies + weight_copies[4:]:
        copy.start()

    for copy in row_copies:
        copy.wait()
    for i in range(4):
        weight_copies[i].wait()
        for part in range(0, parts, 4):
            product = dot(rows_ref[part : part + 4].reshape(4 * rows, enc), weight_refs[i][...]).astype(BF16)
            kv_ref[part : part + 4, :, :, i * half : (i + 1) * half] = product.reshape((4,) + kv_ref.shape[1:3] + (half,))

    for copy in query_copies:
        copy.wait()
    is_first_row = lax.broadcasted_iota(jnp.int32, (CL, HS), 0) == 0
    heads = [(side, lower) for side in (0, 1) for lower in range(0, half, HS)]

    def attend_span(span, carry):
        crosses = (span == N_Z - 1) & (place_ref[N_Z] == 1)
        scores = []
        for side, lower in heads:
            place = slice(side * half + lower, side * half + lower + HS)
            q = jnp.where(is_first_row | jnp.logical_not(crosses), q_ref[span, :, place], crossing_ref[:, place])
            start = 2 * side * half + lower
            k = kv_ref[:, span, :, start : start + HS].reshape(-1, HS)
            scores.append(lax.dot_general(q, k, (((1,), (1,)), ((), ())), preferred_element_type=F32))
        probs = []
        for score in scores:
            score = score * (1.0 / math.sqrt(HS))
            weights = jnp.exp(score - jnp.max(score, axis=-1, keepdims=True))
            total = jnp.sum(weights, axis=-1, keepdims=True)
            probs.append((weights * (1.0 / total)).astype(BF16))
        for (side, lower), prob in zip(heads, probs):
            start = (2 * side + 1) * half + lower
            v = kv_ref[:, span, :, start : start + HS].reshape(-1, HS)
            context_ref[span, :, side * half + lower : side * half + lower + HS] = dot(prob, v).astype(BF16)
        return carry

    lax.fori_loop(0, N_Z, attend_span, 0)

    for copy in weight_copies[4:]:
        copy.wait()
    context = jnp.concatenate([context_ref[place_ref[i]] for i in range(N_Z)], axis=0)
    tile = model // 4
    for lower in range(0, model, tile):
        place = slice(lower, lower + tile)
        product = dot(context[:, :half], weight_refs[4][:, place]) + dot(context[:, half:], weight_refs[5][:, place])
        product = product.astype(BF16)
        side, start = lower // (model // 2), lower % (model // 2)
        for i in range(N_Z):
            out_refs[2 * i + side][:, start : start + tile] = product[i * CL : (i + 1) * CL]
        if start + tile == model // 2:
            for i in range(side, 2 * N_Z, 2):
                pltpu.make_async_copy(out_refs[i], out_hbm[i], out_sem.at[i]).start()
    for i in range(2 * N_Z):
        pltpu.make_async_copy(out_refs[i], out_hbm[i], out_sem.at[i]).wait()


def attend(places, queries, crossing, parts, weights):
    spans, tokens, width = queries.shape
    half, model = weights[4].shape
    rows, enc = parts[0].shape
    out = jax.ShapeDtypeStruct((tokens, model // 2), BF16)
    return pl.pallas_call(
        span_kernel,
        grid_spec=pltpu.PrefetchScalarGridSpec(
            num_scalar_prefetch=1,
            grid=(1,),
            in_specs=[pl.BlockSpec(memory_space=pltpu.HBM)] * 16,
            out_specs=[pl.BlockSpec(memory_space=pltpu.HBM)] * 8,
            scratch_shapes=[pltpu.VMEM(out.shape, BF16)] * 8
            + [
                pltpu.VMEM(queries.shape, BF16),
                pltpu.VMEM(crossing.shape, BF16),
                pltpu.VMEM((len(parts), rows, enc), BF16),
            ]
            + [pltpu.VMEM(weight.shape, BF16) for weight in weights]
            + [
                pltpu.VMEM((len(parts), spans, rows // spans, 4 * half), BF16),
                pltpu.VMEM(queries.shape, BF16),
                pltpu.SemaphoreType.DMA((16,)),
                pltpu.SemaphoreType.DMA((8,)),
            ],
        ),
        out_shape=[out] * 8,
        cost_estimate=cost(5e9),
        compiler_params=pltpu.CompilerParams(vmem_limit_bytes=LIMIT),
    )(places, queries, crossing, *parts, *weights)


def body(decoder, w_query, w_key, w_value, w_out, database, nb_shard, nb_slot):
    n_seq = lax.axis_size("seq")
    seq_index, z_index, core = lax.axis_index("seq"), lax.axis_index("z"), lax.axis_index("core")
    tok_rows, model = decoder.shape
    spans = tok_rows // CL
    requests = NEIGH * spans
    capacity = (requests + n_seq - 1) // n_seq + 1
    slots, _, enc = database.shape
    piece = NB_LEN // (N_Z * N_CORE)

    bits = (slots - 1).bit_length()
    lists = (nb_shard.T << bits) + nb_slot.T
    lists = lists.reshape(NEIGH, n_seq, spans).transpose(1, 0, 2).reshape(n_seq, requests)
    shard_lists, slot_lists = lists >> bits, lists & ((1 << bits) - 1)
    places = bucket_places(shard_lists)
    picked = (shard_lists == seq_index)[:, None, :] & (places[:, None, :] == jnp.arange(capacity)[None, :, None])
    send_slot = jnp.sum(jnp.where(picked, slot_lists[:, None, :], 0), axis=2)
    (outgoing,) = pick(database, send_slot.reshape(-1), z_index * N_CORE + core, piece, [n_seq * capacity])
    received = lax.all_to_all(
        outgoing.reshape(n_seq, capacity, piece, enc), "seq", split_axis=0, concat_axis=0, tiled=True
    )
    received = received.reshape(n_seq * capacity, piece, enc)

    w_query_other = step(w_query, "core", 1)
    weights = (w_key, w_value, *(step(weight, "core", 1) for weight in (w_key, w_value)), w_out, step(w_out, "core", 1))
    first_queries, second_queries, crossing = project_queries(decoder, w_query, w_query_other, core)
    received, weights, crossing = lax.optimization_barrier((received, weights, crossing))

    my_shards = lax.dynamic_index_in_dim(shard_lists, seq_index, 0, keepdims=False)
    my_places = lax.dynamic_index_in_dim(places, seq_index, 0, keepdims=False)
    row_index = (my_shards * capacity + my_places).reshape(NEIGH, N_Z, N_CORE, 2)
    row_index = row_index.transpose(2, 3, 1, 0)[:, ::-1]
    row_index = jnp.where(core == 0, row_index, row_index[::-1]).reshape(-1)
    group = row_index.shape[0] // 4
    mine_a, mine_b, theirs_a, theirs_b = [
        rows.reshape(-1, enc) for rows in pick(received, row_index, jnp.zeros((), jnp.int32), piece, [group] * 4)
    ]

    def hop(value, steps, cross):
        pairs = [
            (z * N_CORE + c, (z + steps) % N_Z * N_CORE + (c + cross) % N_CORE)
            for z in range(N_Z)
            for c in range(N_CORE)
        ]
        return lax.ppermute(value, ("z", "core"), pairs)

    def neighbours(mine, theirs):
        return [hop(mine, 1, 0), hop(theirs, -1, 1), hop(theirs, 1, 1), hop(mine, -1, 0)]

    def opposite(ring):
        return hop(ring[0], 1, 0), hop(ring[1], -1, 0)

    def add(*terms):
        return sum(term.astype(F32) for term in terms).astype(BF16)

    def total(here, down_left, up_left, up_right, down_right):
        return jnp.concatenate([add(here[0], down_left, up_left), add(here[1], up_right, down_right)], axis=1)

    distance = jnp.array([2, 1, 3, 0], jnp.int32)
    places_a = jnp.append((z_index + distance + (N_Z - 1) * core) % N_Z, core).astype(jnp.int32)
    places_b = jnp.append((z_index + distance) % N_Z, 0).astype(jnp.int32)

    ring_a, swapped_a = neighbours(mine_a, theirs_a), hop(theirs_a, 0, 1)
    ring_a, swapped_a, crossing, mine_b, theirs_b = lax.optimization_barrier(
        (ring_a, swapped_a, crossing, mine_b, theirs_b)
    )
    far_a = opposite(ring_a)
    ring_b, swapped_b = neighbours(mine_b, theirs_b), hop(theirs_b, 0, 1)
    crossing = lax.ppermute(crossing, ("seq", "core"), [(2 * i + 2, 2 * i + 1) for i in range(n_seq - 1)])
    far_a, crossing, ring_b, swapped_b = lax.optimization_barrier((far_a, crossing, ring_b, swapped_b))

    far_b = opposite(ring_b)
    sums_a = attend(places_a, second_queries, crossing, (mine_a, swapped_a, *ring_a, *far_a), weights)
    sums_a, far_b = lax.optimization_barrier((sums_a, far_b))
    up_a, down_a = step(sums_a[0], "z", 1), step(sums_a[1], "z", -1)
    up_right_a, down_left_a = step(sums_a[3], "z", 1), step(sums_a[4], "z", -1)
    sums_b = attend(places_b, first_queries, crossing, (mine_b, swapped_b, *ring_b, *far_b), weights)
    sums_b, up_a, down_a = lax.optimization_barrier((sums_b, up_a, down_a))
    up_left_a, down_right_a = step(add(sums_a[2], up_a), "z", 1), step(add(sums_a[5], down_a), "z", -1)
    up_b, down_b = step(sums_b[0], "z", 1), step(sums_b[1], "z", -1)
    up_right_b, down_left_b = step(sums_b[3], "z", 1), step(sums_b[4], "z", -1)
    up_left_b, down_right_b = step(add(sums_b[2], up_b), "z", 1), step(add(sums_b[5], down_b), "z", -1)

    out_a = total(sums_a[6:], down_left_a, up_left_a, up_right_a, down_right_a)
    last = lax.ppermute(out_a[:1], ("z", "core"), [(2 * z + 1, (2 * z - 1) % (N_Z * N_CORE)) for z in range(N_Z)])
    last = jnp.where(core == 0, out_a[:1], last)
    pairs = []
    for i in range(0, n_seq * N_Z * N_CORE, 2):
        pairs.append((i, i + 1))
        if i % (N_Z * N_CORE):
            pairs.append((i + 1, i))
        elif i + N_Z * N_CORE < n_seq * N_Z * N_CORE:
            pairs.append((i + 1, i + N_Z * N_CORE))
    head = lax.ppermute(out_a, ("seq", "z", "core"), pairs)
    out_b = total(sums_b[6:], down_left_b, up_left_b, up_right_b, down_right_b)
    return jnp.concatenate([head[1:], out_b, last], axis=0)


def solution(mesh):
    n_seq = mesh.devices.shape[0]
    fine = Mesh(mesh.devices.reshape(n_seq, N_Z, N_CORE), ("seq", "z", "core"))
    db = ("z", "core")
    return jax.shard_map(
        body,
        mesh=fine,
        in_specs=(
            P("seq", None),
            P(None, db),
            P(None, db),
            P(None, db),
            P(db, None),
            P("seq", None, None),
            P(),
            P(),
        ),
        out_specs=P(("seq", "z", "core"), None),
        check_vma=False,
    )
```

```python
import functools
import math

import jax
import jax.numpy as jnp
from jax import lax
from jax.experimental import pallas as pl
from jax.experimental.pallas import tpu as pltpu
from jax.sharding import Mesh, PartitionSpec as P

HS = 128
CL = 64
NB_LEN = 128
NEIGH = 2
N_Z = 4
N_CORE = 2
BLOCK = 128
F32 = jnp.float32
BF16 = jnp.bfloat16
SHARE = 0.4
LIMIT = 60 * 1024 * 1024


def step(value, axis, steps):
    count = lax.axis_size(axis)
    return lax.ppermute(value, axis, [(i, (i + steps) % count) for i in range(count)])


def cost(flops):
    return pl.CostEstimate(flops=int(flops * SHARE), bytes_accessed=int(flops * SHARE / 1000), transcendentals=0)


def dot(a, b):
    return jnp.dot(a, b, preferred_element_type=F32)


def bucket_places(shards):
    count = shards.shape[1]
    same_shard = shards[:, :, None] == shards[:, None, :]
    earlier = jnp.arange(count)[None, :] < jnp.arange(count)[:, None]
    return jnp.sum((same_shard & earlier[None]).astype(jnp.int32), axis=2)


def pick_kernel(index_ref, start_ref, source_ref, *refs):
    out_refs, rows_ref, sem = refs[:-2], refs[-2], refs[-1]
    rows = rows_ref.shape[1]
    start = pl.multiple_of(start_ref[0] * rows, rows)
    copy = pltpu.make_async_copy(source_ref.at[:, pl.ds(start, rows)], rows_ref, sem)
    copy.start()
    copy.wait()
    place = 0
    for out_ref in out_refs:
        for i in range(out_ref.shape[0]):
            out_ref[i] = rows_ref[index_ref[place]]
            place += 1


def pick(source, index, start, rows, counts):
    shapes = [(count, rows, source.shape[2]) for count in counts]
    return pl.pallas_call(
        pick_kernel,
        grid_spec=pltpu.PrefetchScalarGridSpec(
            num_scalar_prefetch=2,
            grid=(1,),
            in_specs=[pl.BlockSpec(memory_space=pltpu.HBM)],
            out_specs=[pl.BlockSpec(shape, lambda i, index, start: (0, 0, 0)) for shape in shapes],
            scratch_shapes=[pltpu.VMEM((source.shape[0], rows, source.shape[2]), source.dtype), pltpu.SemaphoreType.DMA],
        ),
        out_shape=[jax.ShapeDtypeStruct(shape, source.dtype) for shape in shapes],
        cost_estimate=cost(1e9),
        compiler_params=pltpu.CompilerParams(vmem_limit_bytes=LIMIT),
    )(index, start.reshape(1), source)


def query_kernel(core_ref, x_hbm, wa_hbm, wb_hbm, first_ref, second_ref, crossing_ref, x_ref, wa_ref, wb_ref, sems):
    half = wa_ref.shape[1]
    copies = []
    for j in range(N_Z):
        block = N_CORE * j + core_ref[0]
        after = lax.rem(block + 1, N_Z * N_CORE)
        copies.append(pltpu.make_async_copy(x_hbm.at[block], x_ref.at[j, :BLOCK], sems.at[2 * j]))
        copies.append(pltpu.make_async_copy(x_hbm.at[after, :CL], x_ref.at[j, BLOCK:], sems.at[2 * j + 1]))
    copies.append(pltpu.make_async_copy(wa_hbm, wa_ref, sems.at[2 * N_Z]))
    copies.append(pltpu.make_async_copy(wb_hbm, wb_ref, sems.at[2 * N_Z + 1]))
    for copy in copies:
        copy.start()
    for j in range(N_Z):
        copies[2 * j].wait()
        copies[2 * j + 1].wait()
        source = x_ref[j].astype(F32)
        scale = lax.rsqrt(jnp.mean(source * source, axis=-1, keepdims=True) + 1e-05)
        x_ref[j] = (source * scale).astype(BF16)
    rows = BLOCK + CL
    for i, weight_ref in enumerate((wa_ref, wb_ref)):
        copies[2 * N_Z + i].wait()
        here, there = slice(i * half, (i + 1) * half), slice((1 - i) * half, (2 - i) * half)
        product = dot(x_ref[...].reshape(N_Z * rows, -1), weight_ref[...])
        for j in range(N_Z):
            rolled = pltpu.roll(product[j * rows : (j + 1) * rows], 1, 0).astype(BF16)
            first_ref[j, :, here] = rolled[CL:BLOCK]
            second_ref[j, :, here] = rolled[BLOCK:]
            if j == 0:
                crossing_ref[:, there] = rolled[:CL]


def project_queries(decoder, weight_a, weight_b, core):
    model, half = weight_a.shape
    blocks = decoder.reshape(N_Z * N_CORE, BLOCK, model)
    shape = (N_Z, CL, 2 * half)
    out_spec = pl.BlockSpec(shape, lambda i, core: (0, 0, 0))
    return pl.pallas_call(
        query_kernel,
        grid_spec=pltpu.PrefetchScalarGridSpec(
            num_scalar_prefetch=1,
            grid=(1,),
            in_specs=[pl.BlockSpec(memory_space=pltpu.HBM)] * 3,
            out_specs=[out_spec, out_spec, pl.BlockSpec(shape[1:], lambda i, core: (0, 0))],
            scratch_shapes=[
                pltpu.VMEM((N_Z, BLOCK + CL, model), BF16),
                pltpu.VMEM((model, half), BF16),
                pltpu.VMEM((model, half), BF16),
                pltpu.SemaphoreType.DMA((2 * N_Z + 2,)),
            ],
        ),
        out_shape=[jax.ShapeDtypeStruct(dims, BF16) for dims in (shape, shape, shape[1:])],
        cost_estimate=cost(3e9),
        compiler_params=pltpu.CompilerParams(vmem_limit_bytes=LIMIT),
    )(core.reshape(1), blocks, weight_a, weight_b)


def project_kernel(*refs):
    row_hbm, weight_hbm, out_hbm = refs[:6], refs[6:10], refs[10:14]
    rows_ref, weight_refs, out_refs, sems = refs[14], refs[15:19], refs[19:23], refs[23]
    parts, rows, enc = rows_ref.shape
    row_copies = [pltpu.make_async_copy(row_hbm[i], rows_ref.at[i], sems.at[i]) for i in range(parts)]
    weight_copies = [pltpu.make_async_copy(weight_hbm[i], weight_refs[i], sems.at[parts + i]) for i in range(4)]
    out_copies = [pltpu.make_async_copy(out_refs[i], out_hbm[i], sems.at[parts + 4 + i]) for i in range(4)]
    for copy in row_copies + weight_copies:
        copy.start()
    for copy in row_copies:
        copy.wait()
    for i in range(4):
        weight_copies[i].wait()
        for part in range(0, parts, 2):
            product = dot(rows_ref[part : part + 2].reshape(2 * rows, enc), weight_refs[i][...]).astype(BF16)
            out_refs[i][part : part + 2] = product.reshape((2,) + out_refs[i].shape[1:])
        out_copies[i].start()
    for copy in out_copies:
        copy.wait()


def project(weights, parts):
    rows, enc = parts[0].shape
    width = weights[0].shape[1]
    shape = (len(parts), 2, N_Z, rows // (2 * N_Z), width)
    return pl.pallas_call(
        project_kernel,
        in_specs=[pl.BlockSpec(memory_space=pltpu.HBM)] * (len(parts) + 4),
        out_specs=[pl.BlockSpec(memory_space=pltpu.HBM)] * 4,
        out_shape=[jax.ShapeDtypeStruct(shape, BF16)] * 4,
        scratch_shapes=[pltpu.VMEM((len(parts), rows, enc), BF16)]
        + [pltpu.VMEM((enc, width), BF16)] * 4
        + [pltpu.VMEM(shape, BF16)] * 4
        + [pltpu.SemaphoreType.DMA((len(parts) + 8,))],
        cost_estimate=cost(2e9),
        compiler_params=pltpu.CompilerParams(vmem_limit_bytes=LIMIT),
    )(*parts, *weights)


def span_kernel(group, place_ref, *refs):
    refs = list(refs)

    def take(count):
        taken = refs[:count]
        del refs[:count]
        return taken

    near_hbm, far_hbm = take(4), take(6 if group == 0 else 4)
    q_hbm, crossing_hbm = take(2)
    out_weight_hbm, out_hbm = take(2), take(6)
    later_hbm = take(4 if group == 0 else 0)
    kv_refs, out_refs, out_weight_refs = take(4), take(6), take(2)
    q_ref, crossing_ref, context_ref = take(3)
    rows_ref, *weight_refs = take(5 if group == 0 else 0) or [None]
    later_refs = take(4 if group == 0 else 0)
    in_sems, out_sems = refs
    used = [0, 0]

    def copy_in(source, target):
        used[0] += 1
        return pltpu.make_async_copy(source, target, in_sems.at[used[0] - 1])

    def copy_out(source, target):
        used[1] += 1
        return pltpu.make_async_copy(source, target, out_sems.at[used[1] - 1])

    half, model = out_weight_refs[0].shape
    parts = near_hbm[0].shape[0]
    if group == 0:
        far_copies = [copy_in(far_hbm[i], rows_ref.at[i]) for i in range(2)]
        weight_copies = [copy_in(far_hbm[2 + i], weight_refs[i]) for i in range(4)]
    else:
        far_copies = [copy_in(far_hbm[i], kv_refs[i].at[parts:]) for i in range(4)]
        weight_copies = []
    near_copies = [copy_in(near_hbm[i].at[:, group], kv_refs[i].at[:parts]) for i in range(4)]
    query_copies = [copy_in(q_hbm, q_ref), copy_in(crossing_hbm, crossing_ref)]
    out_weight_copies = [copy_in(out_weight_hbm[i], out_weight_refs[i]) for i in range(2)]
    for copy in far_copies + weight_copies + near_copies + query_copies + out_weight_copies:
        copy.start()
    for copy in far_copies:
        copy.wait()
    later_copies = []
    for i, copy in enumerate(weight_copies):
        copy.wait()
        product = dot(rows_ref[...].reshape(-1, rows_ref.shape[2]), weight_refs[i][...]).astype(BF16)
        product = product.reshape(2, 2, *kv_refs[i].shape[1:])
        kv_refs[i][parts:] = product[:, 0]
        later_refs[i][...] = product[:, 1]
        later_copies.append(copy_out(later_refs[i], later_hbm[i]))
        later_copies[i].start()
    for copy in near_copies + query_copies:
        copy.wait()

    is_first_row = lax.broadcasted_iota(jnp.int32, (CL, HS), 0) == 0
    heads = [(side, lower) for side in (0, 1) for lower in range(0, half, HS)]

    def attend_span(span, carry):
        crosses = (span == N_Z - 1) & (place_ref[N_Z] == 1)
        scores = []
        for side, lower in heads:
            place = slice(side * half + lower, side * half + lower + HS)
            q = q_ref[span, :, place]
            if group == 0:
                q = jnp.where(is_first_row | jnp.logical_not(crosses), q, crossing_ref[:, place])
            k = kv_refs[2 * side][:, span, :, lower : lower + HS].reshape(-1, HS)
            scores.append(lax.dot_general(q, k, (((1,), (1,)), ((), ())), preferred_element_type=F32))
        probs = []
        for score in scores:
            score = score * (1.0 / math.sqrt(HS))
            weights = jnp.exp(score - jnp.max(score, axis=-1, keepdims=True))
            total = jnp.sum(weights, axis=-1, keepdims=True)
            probs.append((weights * (1.0 / total)).astype(BF16))
        for (side, lower), prob in zip(heads, probs):
            v = kv_refs[2 * side + 1][:, span, :, lower : lower + HS].reshape(-1, HS)
            context_ref[span, :, side * half + lower : side * half + lower + HS] = dot(prob, v).astype(BF16)
        return carry

    lax.fori_loop(0, N_Z, attend_span, 0)

    for copy in out_weight_copies:
        copy.wait()
    context = jnp.concatenate([context_ref[place_ref[i]] for i in range(N_Z)], axis=0)
    up, down, above, below, here_left, here_right = out_refs
    tile = model // 4
    out_copies = [copy_out(out_refs[i], out_hbm[i]) for i in range(6)]
    for lower in range(0, model, tile):
        place = slice(lower, lower + tile)
        product = dot(context[:, :half], out_weight_refs[0][:, place])
        product = (product + dot(context[:, half:], out_weight_refs[1][:, place])).astype(BF16)
        blocks = [product[i * CL : (i + 1) * CL] for i in range(N_Z)]
        inner = slice(lower % (model // 2), lower % (model // 2) + tile)
        if lower < model // 2:
            up[:, place], down[:, place], above[:, inner], here_left[:, inner] = blocks[0], blocks[2], blocks[1], blocks[3]
        else:
            up[:, place], down[:, place], below[:, inner], here_right[:, inner] = blocks[1], blocks[0], blocks[2], blocks[3]
        if lower + tile == model // 2:
            out_copies[2].start()
            out_copies[4].start()
    for i in (0, 1, 3, 5):
        out_copies[i].start()
    for copy in later_copies + out_copies:
        copy.wait()


def attend(group, places, queries, crossing, near, far, out_weights):
    spans, tokens, width = queries.shape
    half, model = out_weights[0].shape
    parts, _, _, rows, _ = near[0].shape
    outs = [(tokens, model)] * 2 + [(tokens, model // 2)] * 4
    scratch = [(parts + 2, spans, rows, half)] * 4 + outs + [(half, model)] * 2
    scratch += [queries.shape, crossing.shape, queries.shape]
    later = [(2, spans, rows, half)] * 4 if group == 0 else []
    if group == 0:
        scratch += [(2,) + far[0].shape] + [weight.shape for weight in far[2:]] + later
    operands = (*near, *far, queries, crossing, *out_weights)
    return pl.pallas_call(
        functools.partial(span_kernel, group),
        grid_spec=pltpu.PrefetchScalarGridSpec(
            num_scalar_prefetch=1,
            grid=(1,),
            in_specs=[pl.BlockSpec(memory_space=pltpu.HBM)] * len(operands),
            out_specs=[pl.BlockSpec(memory_space=pltpu.HBM)] * (6 + len(later)),
            scratch_shapes=[pltpu.VMEM(shape, BF16) for shape in scratch]
            + [pltpu.SemaphoreType.DMA((len(operands),)), pltpu.SemaphoreType.DMA((6 + len(later),))],
        ),
        out_shape=[jax.ShapeDtypeStruct(shape, BF16) for shape in outs + later],
        cost_estimate=cost(5e9),
        compiler_params=pltpu.CompilerParams(vmem_limit_bytes=LIMIT),
    )(places, *operands)


def body(decoder, w_query, w_key, w_value, w_out, database, nb_shard, nb_slot):
    n_seq = lax.axis_size("seq")
    seq_index, z_index, core = lax.axis_index("seq"), lax.axis_index("z"), lax.axis_index("core")
    tok_rows, model = decoder.shape
    spans = tok_rows // CL
    requests = NEIGH * spans
    capacity = (requests + n_seq - 1) // n_seq + 1
    slots, _, enc = database.shape
    piece = NB_LEN // (N_Z * N_CORE)

    bits = (slots - 1).bit_length()
    lists = (nb_shard.T << bits) + nb_slot.T
    lists = lists.reshape(NEIGH, n_seq, spans).transpose(1, 0, 2).reshape(n_seq, requests)
    shard_lists, slot_lists = lists >> bits, lists & ((1 << bits) - 1)
    places = bucket_places(shard_lists)
    picked = (shard_lists == seq_index)[:, None, :] & (places[:, None, :] == jnp.arange(capacity)[None, :, None])
    send_slot = jnp.sum(jnp.where(picked, slot_lists[:, None, :], 0), axis=2)
    (outgoing,) = pick(database, send_slot.reshape(-1), z_index * N_CORE + core, piece, [n_seq * capacity])
    received = lax.all_to_all(
        outgoing.reshape(n_seq, capacity, piece, enc), "seq", split_axis=0, concat_axis=0, tiled=True
    )
    received = received.reshape(n_seq * capacity, piece, enc)

    w_query_other = step(w_query, "core", 1)
    weights = (w_key, w_value, *(step(weight, "core", 1) for weight in (w_key, w_value)), w_out, step(w_out, "core", 1))
    first_queries, second_queries, crossing = project_queries(decoder, w_query, w_query_other, core)
    received, weights, crossing = lax.optimization_barrier((received, weights, crossing))

    my_shards = lax.dynamic_index_in_dim(shard_lists, seq_index, 0, keepdims=False)
    my_places = lax.dynamic_index_in_dim(places, seq_index, 0, keepdims=False)
    row_index = (my_shards * capacity + my_places).reshape(NEIGH, N_Z, N_CORE, 2)
    row_index = row_index.transpose(2, 3, 1, 0)[:, ::-1]
    row_index = jnp.where(core == 0, row_index, row_index[::-1]).reshape(-1)
    count = row_index.shape[0] // 2
    mine, theirs = pick(received, row_index, jnp.zeros((), jnp.int32), piece, [count] * 2)
    mine, theirs = mine.reshape(-1, enc), theirs.reshape(-1, enc)

    def hop(value, steps, cross):
        pairs = [
            (z * N_CORE + c, (z + steps) % N_Z * N_CORE + (c + cross) % N_CORE)
            for z in range(N_Z)
            for c in range(N_CORE)
        ]
        return lax.ppermute(value, ("z", "core"), pairs)

    def add(*terms):
        return sum(term.astype(F32) for term in terms).astype(BF16)

    side = model // 2

    def total(here_left, here_right, up, down, up_left, down_right):
        left, right = add(here_left, down[:, :side], up_left), add(here_right, up[:, side:], down_right)
        return jnp.concatenate([left, right], axis=1)

    distance = jnp.array([2, 1, 3, 0], jnp.int32)
    places_a = jnp.append((z_index + distance + (N_Z - 1) * core) % N_Z, core).astype(jnp.int32)
    places_b = jnp.append((z_index + distance) % N_Z, 0).astype(jnp.int32)

    ring = [hop(mine, 1, 0), hop(theirs, -1, 1), hop(theirs, 1, 1), hop(mine, -1, 0)]
    swapped = hop(theirs, 0, 1)
    ring, swapped, crossing, places_a, places_b = lax.optimization_barrier(
        (ring, swapped, crossing, places_a, places_b)
    )
    far = hop(ring[0], 1, 0), hop(ring[1], -1, 0)
    crossing = lax.ppermute(crossing, ("seq", "core"), [(2 * i + 2, 2 * i + 1) for i in range(n_seq - 1)])
    near = project(weights[:4], (mine, swapped, *ring))

    up_a, down_a, above_a, below_a, *rest = attend(
        0, places_a, second_queries, crossing, near, (*far, *weights[:4]), weights[4:]
    )
    here_a, far = rest[:2], rest[2:]
    up_a, down_a = step(up_a, "z", 1), step(down_a, "z", -1)
    up_b, down_b, above_b, below_b, *here_b = attend(1, places_b, first_queries, crossing, near, far, weights[4:])
    up_a, down_a, up_b, down_b = lax.optimization_barrier((up_a, down_a, up_b, down_b))
    above_a, below_a = lax.optimization_barrier((add(above_a, up_a[:, :side]), add(below_a, down_a[:, side:])))
    up_left_a, down_right_a = step(above_a, "z", 1), step(below_a, "z", -1)
    up_b, down_b = step(up_b, "z", 1), step(down_b, "z", -1)
    out_a = total(*here_a, up_a, down_a, up_left_a, down_right_a)
    out_a, up_b, down_b = lax.optimization_barrier((out_a, up_b, down_b))
    above_b, below_b = lax.optimization_barrier((add(above_b, up_b[:, :side]), add(below_b, down_b[:, side:])))
    up_left_b, down_right_b = step(above_b, "z", 1), step(below_b, "z", -1)

    last = lax.ppermute(out_a[:1], ("z", "core"), [(2 * z + 1, (2 * z - 1) % (N_Z * N_CORE)) for z in range(N_Z)])
    last = jnp.where(core == 0, out_a[:1], last)
    pairs = []
    for i in range(0, n_seq * N_Z * N_CORE, 2):
        pairs.append((i, i + 1))
        if i % (N_Z * N_CORE):
            pairs.append((i + 1, i))
        elif i + N_Z * N_CORE < n_seq * N_Z * N_CORE:
            pairs.append((i + 1, i + N_Z * N_CORE))
    head = lax.ppermute(out_a, ("seq", "z", "core"), pairs)
    out_b = total(*here_b, up_b, down_b, up_left_b, down_right_b)
    return jnp.concatenate([head[1:], out_b, last], axis=0)


def solution(mesh):
    n_seq = mesh.devices.shape[0]
    fine = Mesh(mesh.devices.reshape(n_seq, N_Z, N_CORE), ("seq", "z", "core"))
    db = ("z", "core")
    return jax.shard_map(
        body,
        mesh=fine,
        in_specs=(
            P("seq", None),
            P(None, db),
            P(None, db),
            P(None, db),
            P(db, None),
            P("seq", None, None),
            P(),
            P(),
        ),
        out_specs=P(("seq", "z", "core"), None),
        check_vma=False,
    )
```

```python
import functools
import math

import jax
import jax.numpy as jnp
from jax import lax
from jax.experimental import pallas as pl
from jax.experimental.pallas import tpu as pltpu
from jax.sharding import Mesh, PartitionSpec as P

HS = 128
CL = 64
NB_LEN = 128
NEIGH = 2
N_Z = 4
N_CORE = 2
BLOCK = 128
F32 = jnp.float32
BF16 = jnp.bfloat16
SHARE = 0.4
LIMIT = 60 * 1024 * 1024


def step(value, axis, steps):
    count = lax.axis_size(axis)
    return lax.ppermute(value, axis, [(i, (i + steps) % count) for i in range(count)])


def cost(flops):
    return pl.CostEstimate(flops=int(flops * SHARE), bytes_accessed=int(flops * SHARE / 1000), transcendentals=0)


def dot(a, b):
    return jnp.dot(a, b, preferred_element_type=F32)


def bucket_places(shards):
    count = shards.shape[1]
    same_shard = shards[:, :, None] == shards[:, None, :]
    earlier = jnp.arange(count)[None, :] < jnp.arange(count)[:, None]
    return jnp.sum((same_shard & earlier[None]).astype(jnp.int32), axis=2)


def pick_kernel(index_ref, start_ref, source_ref, *refs):
    out_refs, rows_ref, sem = refs[:-2], refs[-2], refs[-1]
    rows = rows_ref.shape[1]
    start = pl.multiple_of(start_ref[0] * rows, rows)
    copy = pltpu.make_async_copy(source_ref.at[:, pl.ds(start, rows)], rows_ref, sem)
    copy.start()
    copy.wait()
    place = 0
    for out_ref in out_refs:
        for i in range(out_ref.shape[0]):
            out_ref[i] = rows_ref[index_ref[place]]
            place += 1


def pick(source, index, start, rows, counts):
    shapes = [(count, rows, source.shape[2]) for count in counts]
    return pl.pallas_call(
        pick_kernel,
        grid_spec=pltpu.PrefetchScalarGridSpec(
            num_scalar_prefetch=2,
            grid=(1,),
            in_specs=[pl.BlockSpec(memory_space=pltpu.HBM)],
            out_specs=[pl.BlockSpec(shape, lambda i, index, start: (0, 0, 0)) for shape in shapes],
            scratch_shapes=[pltpu.VMEM((source.shape[0], rows, source.shape[2]), source.dtype), pltpu.SemaphoreType.DMA],
        ),
        out_shape=[jax.ShapeDtypeStruct(shape, source.dtype) for shape in shapes],
        cost_estimate=cost(1e9),
        compiler_params=pltpu.CompilerParams(vmem_limit_bytes=LIMIT),
    )(index, start.reshape(1), source)


def query_kernel(core_ref, x_hbm, wa_hbm, wb_hbm, first_ref, second_ref, crossing_ref, x_ref, wa_ref, wb_ref, sems):
    half = wa_ref.shape[1]
    copies = []
    for j in range(N_Z):
        block = N_CORE * j + core_ref[0]
        after = lax.rem(block + 1, N_Z * N_CORE)
        copies.append(pltpu.make_async_copy(x_hbm.at[block], x_ref.at[j, :BLOCK], sems.at[2 * j]))
        copies.append(pltpu.make_async_copy(x_hbm.at[after, :CL], x_ref.at[j, BLOCK:], sems.at[2 * j + 1]))
    copies.append(pltpu.make_async_copy(wa_hbm, wa_ref, sems.at[2 * N_Z]))
    copies.append(pltpu.make_async_copy(wb_hbm, wb_ref, sems.at[2 * N_Z + 1]))
    for copy in copies:
        copy.start()
    for j in range(N_Z):
        copies[2 * j].wait()
        copies[2 * j + 1].wait()
        source = x_ref[j].astype(F32)
        scale = lax.rsqrt(jnp.mean(source * source, axis=-1, keepdims=True) + 1e-05)
        x_ref[j] = (source * scale).astype(BF16)
    rows = BLOCK + CL
    for i, weight_ref in enumerate((wa_ref, wb_ref)):
        copies[2 * N_Z + i].wait()
        here, there = slice(i * half, (i + 1) * half), slice((1 - i) * half, (2 - i) * half)
        product = dot(x_ref[...].reshape(N_Z * rows, -1), weight_ref[...])
        for j in range(N_Z):
            rolled = pltpu.roll(product[j * rows : (j + 1) * rows], 1, 0).astype(BF16)
            first_ref[j, :, here] = rolled[CL:BLOCK]
            second_ref[j, :, here] = rolled[BLOCK:]
            if j == 0:
                crossing_ref[:, there] = rolled[:CL]


def project_queries(decoder, weight_a, weight_b, core):
    model, half = weight_a.shape
    blocks = decoder.reshape(N_Z * N_CORE, BLOCK, model)
    shape = (N_Z, CL, 2 * half)
    out_spec = pl.BlockSpec(shape, lambda i, core: (0, 0, 0))
    return pl.pallas_call(
        query_kernel,
        grid_spec=pltpu.PrefetchScalarGridSpec(
            num_scalar_prefetch=1,
            grid=(1,),
            in_specs=[pl.BlockSpec(memory_space=pltpu.HBM)] * 3,
            out_specs=[out_spec, out_spec, pl.BlockSpec(shape[1:], lambda i, core: (0, 0))],
            scratch_shapes=[
                pltpu.VMEM((N_Z, BLOCK + CL, model), BF16),
                pltpu.VMEM((model, half), BF16),
                pltpu.VMEM((model, half), BF16),
                pltpu.SemaphoreType.DMA((2 * N_Z + 2,)),
            ],
        ),
        out_shape=[jax.ShapeDtypeStruct(dims, BF16) for dims in (shape, shape, shape[1:])],
        cost_estimate=cost(3e9),
        compiler_params=pltpu.CompilerParams(vmem_limit_bytes=LIMIT),
    )(core.reshape(1), blocks, weight_a, weight_b)


def project_kernel(*refs):
    row_hbm, weight_hbm, out_hbm = refs[:-18], refs[-18:-14], refs[-14:-10]
    rows_ref, weight_refs, out_refs, sems = refs[-10], refs[-9:-5], refs[-5:-1], refs[-1]
    parts, rows, enc = rows_ref.shape
    row_copies = [pltpu.make_async_copy(row_hbm[i], rows_ref.at[i], sems.at[i]) for i in range(parts)]
    weight_copies = [pltpu.make_async_copy(weight_hbm[i], weight_refs[i], sems.at[parts + i]) for i in range(4)]
    out_copies = [pltpu.make_async_copy(out_refs[i], out_hbm[i], sems.at[parts + 4 + i]) for i in range(4)]
    for copy in row_copies + weight_copies:
        copy.start()
    for copy in row_copies:
        copy.wait()
    for i in range(4):
        weight_copies[i].wait()
        for part in range(0, parts, 2):
            product = dot(rows_ref[part : part + 2].reshape(2 * rows, enc), weight_refs[i][...]).astype(BF16)
            out_refs[i][part : part + 2] = product.reshape((2,) + out_refs[i].shape[1:])
        out_copies[i].start()
    for copy in out_copies:
        copy.wait()


def project(weights, parts):
    rows, enc = parts[0].shape
    width = weights[0].shape[1]
    shape = (len(parts), 2, N_Z, rows // (2 * N_Z), width)
    return pl.pallas_call(
        project_kernel,
        in_specs=[pl.BlockSpec(memory_space=pltpu.HBM)] * (len(parts) + 4),
        out_specs=[pl.BlockSpec(memory_space=pltpu.HBM)] * 4,
        out_shape=[jax.ShapeDtypeStruct(shape, BF16)] * 4,
        scratch_shapes=[pltpu.VMEM((len(parts), rows, enc), BF16)]
        + [pltpu.VMEM((enc, width), BF16)] * 4
        + [pltpu.VMEM(shape, BF16)] * 4
        + [pltpu.SemaphoreType.DMA((len(parts) + 8,))],
        cost_estimate=cost(2e9),
        compiler_params=pltpu.CompilerParams(vmem_limit_bytes=LIMIT),
    )(*parts, *weights)


def span_kernel(group, place_ref, *refs):
    refs = list(refs)

    def take(count):
        taken = refs[:count]
        del refs[:count]
        return taken

    near_hbm, far_hbm = take(8), take(6 if group == 0 else 4)
    q_hbm, crossing_hbm = take(2)
    out_weight_hbm, out_hbm = take(2), take(6)
    later_hbm = take(4 if group == 0 else 0)
    kv_refs, out_refs, out_weight_refs = take(4), take(6), take(2)
    q_ref, crossing_ref, context_ref = take(3)
    rows_ref, *weight_refs = take(5 if group == 0 else 0) or [None]
    later_refs = take(4 if group == 0 else 0)
    in_sems, out_sems = refs
    used = [0, 0]

    def copy_in(source, target):
        used[0] += 1
        return pltpu.make_async_copy(source, target, in_sems.at[used[0] - 1])

    def copy_out(source, target):
        used[1] += 1
        return pltpu.make_async_copy(source, target, out_sems.at[used[1] - 1])

    half, model = out_weight_refs[0].shape
    own, parts = near_hbm[0].shape[0], near_hbm[0].shape[0] + near_hbm[4].shape[0]
    if group == 0:
        far_copies = [copy_in(far_hbm[i], rows_ref.at[i]) for i in range(2)]
        weight_copies = [copy_in(far_hbm[2 + i], weight_refs[i]) for i in range(4)]
    else:
        far_copies = [copy_in(far_hbm[i], kv_refs[i].at[parts:]) for i in range(4)]
        weight_copies = []
    near_copies = [copy_in(near_hbm[i].at[:, group], kv_refs[i].at[:own]) for i in range(4)]
    near_copies += [copy_in(near_hbm[4 + i].at[:, group], kv_refs[i].at[own:parts]) for i in range(4)]
    query_copies = [copy_in(q_hbm, q_ref), copy_in(crossing_hbm, crossing_ref)]
    out_weight_copies = [copy_in(out_weight_hbm[i], out_weight_refs[i]) for i in range(2)]
    for copy in far_copies + weight_copies + near_copies + query_copies + out_weight_copies:
        copy.start()
    for copy in far_copies:
        copy.wait()
    later_copies = []
    for i, copy in enumerate(weight_copies):
        copy.wait()
        product = dot(rows_ref[...].reshape(-1, rows_ref.shape[2]), weight_refs[i][...]).astype(BF16)
        product = product.reshape(2, 2, *kv_refs[i].shape[1:])
        kv_refs[i][parts:] = product[:, 0]
        later_refs[i][...] = product[:, 1]
        later_copies.append(copy_out(later_refs[i], later_hbm[i]))
        later_copies[i].start()
    for copy in near_copies + query_copies:
        copy.wait()

    is_first_row = lax.broadcasted_iota(jnp.int32, (CL, HS), 0) == 0
    heads = [(side, lower) for side in (0, 1) for lower in range(0, half, HS)]

    def attend_span(span, carry):
        crosses = (span == N_Z - 1) & (place_ref[N_Z] == 1)
        scores = []
        for side, lower in heads:
            place = slice(side * half + lower, side * half + lower + HS)
            q = q_ref[span, :, place]
            if group == 0:
                q = jnp.where(is_first_row | jnp.logical_not(crosses), q, crossing_ref[:, place])
            k = kv_refs[2 * side][:, span, :, lower : lower + HS].reshape(-1, HS)
            scores.append(lax.dot_general(q, k, (((1,), (1,)), ((), ())), preferred_element_type=F32))
        probs = []
        for score in scores:
            score = score * (1.0 / math.sqrt(HS))
            weights = jnp.exp(score - jnp.max(score, axis=-1, keepdims=True))
            total = jnp.sum(weights, axis=-1, keepdims=True)
            probs.append((weights * (1.0 / total)).astype(BF16))
        for (side, lower), prob in zip(heads, probs):
            v = kv_refs[2 * side + 1][:, span, :, lower : lower + HS].reshape(-1, HS)
            context_ref[span, :, side * half + lower : side * half + lower + HS] = dot(prob, v).astype(BF16)
        return carry

    lax.fori_loop(0, N_Z, attend_span, 0)

    for copy in out_weight_copies:
        copy.wait()
    blocks = [context_ref[place_ref[i]] for i in range(N_Z)]
    if group == 0:
        is_first_row = lax.broadcasted_iota(jnp.int32, blocks[0].shape, 0) == 0
        blocks = [jnp.where(is_first_row, context_ref[place_ref[N_Z + 1 + i]], blocks[i]) for i in range(N_Z)]
    context = jnp.concatenate(blocks, axis=0)
    up, down, above, below, here_left, here_right = out_refs
    tile = model // 4
    out_copies = [copy_out(out_refs[i], out_hbm[i]) for i in range(6)]
    for lower in range(0, model, tile):
        place = slice(lower, lower + tile)
        product = dot(context[:, :half], out_weight_refs[0][:, place])
        product = (product + dot(context[:, half:], out_weight_refs[1][:, place])).astype(BF16)
        blocks = [product[i * CL : (i + 1) * CL] for i in range(N_Z)]
        inner = slice(lower % (model // 2), lower % (model // 2) + tile)
        if lower < model // 2:
            up[:, place], down[:, place], above[:, inner], here_left[:, inner] = blocks[0], blocks[2], blocks[1], blocks[3]
        else:
            up[:, place], down[:, place], below[:, inner], here_right[:, inner] = blocks[1], blocks[0], blocks[2], blocks[3]
        if lower + tile == model // 2:
            out_copies[2].start()
            out_copies[4].start()
    for i in (0, 1, 3, 5):
        out_copies[i].start()
    for copy in later_copies + out_copies:
        copy.wait()


def attend(group, places, queries, crossing, near, far, out_weights):
    spans, tokens, width = queries.shape
    half, model = out_weights[0].shape
    parts, rows = near[0].shape[0] + near[4].shape[0], near[0].shape[3]
    outs = [(tokens, model)] * 2 + [(tokens, model // 2)] * 4
    scratch = [(parts + 2, spans, rows, half)] * 4 + outs + [(half, model)] * 2
    scratch += [queries.shape, crossing.shape, queries.shape]
    later = [(2, spans, rows, half)] * 4 if group == 0 else []
    if group == 0:
        scratch += [(2,) + far[0].shape] + [weight.shape for weight in far[2:]] + later
    operands = (*near, *far, queries, crossing, *out_weights)
    return pl.pallas_call(
        functools.partial(span_kernel, group),
        grid_spec=pltpu.PrefetchScalarGridSpec(
            num_scalar_prefetch=1,
            grid=(1,),
            in_specs=[pl.BlockSpec(memory_space=pltpu.HBM)] * len(operands),
            out_specs=[pl.BlockSpec(memory_space=pltpu.HBM)] * (6 + len(later)),
            scratch_shapes=[pltpu.VMEM(shape, BF16) for shape in scratch]
            + [pltpu.SemaphoreType.DMA((len(operands),)), pltpu.SemaphoreType.DMA((6 + len(later),))],
        ),
        out_shape=[jax.ShapeDtypeStruct(shape, BF16) for shape in outs + later],
        cost_estimate=cost(5e9),
        compiler_params=pltpu.CompilerParams(vmem_limit_bytes=LIMIT),
    )(places, *operands)


def body(decoder, w_query, w_key, w_value, w_out, database, nb_shard, nb_slot):
    n_seq = lax.axis_size("seq")
    seq_index, z_index, core = lax.axis_index("seq"), lax.axis_index("z"), lax.axis_index("core")
    tok_rows, model = decoder.shape
    spans = tok_rows // CL
    requests = NEIGH * spans
    capacity = (requests + n_seq - 1) // n_seq + 1
    slots, _, enc = database.shape
    piece = NB_LEN // (N_Z * N_CORE)

    bits = (slots - 1).bit_length()
    lists = (nb_shard.T << bits) + nb_slot.T
    lists = lists.reshape(NEIGH, n_seq, spans).transpose(1, 0, 2).reshape(n_seq, requests)
    shard_lists, slot_lists = lists >> bits, lists & ((1 << bits) - 1)
    places = bucket_places(shard_lists)
    picked = (shard_lists == seq_index)[:, None, :] & (places[:, None, :] == jnp.arange(capacity)[None, :, None])
    send_slot = jnp.sum(jnp.where(picked, slot_lists[:, None, :], 0), axis=2)
    (outgoing,) = pick(database, send_slot.reshape(-1), z_index * N_CORE + core, piece, [n_seq * capacity])
    received = lax.all_to_all(
        outgoing.reshape(n_seq, capacity, piece, enc), "seq", split_axis=0, concat_axis=0, tiled=True
    )
    received = received.reshape(n_seq * capacity, piece, enc)

    w_query_other = step(w_query, "core", 1)
    weights = (w_key, w_value, *(step(weight, "core", 1) for weight in (w_key, w_value)), w_out, step(w_out, "core", 1))
    first_queries, second_queries, crossing = project_queries(decoder, w_query, w_query_other, core)
    distance = jnp.array([2, 1, 3, 0], jnp.int32)
    places_b = (z_index + distance) % N_Z
    places_a = (z_index + distance + (N_Z - 1) * core) % N_Z
    places_a = jnp.concatenate([places_a, core.reshape(1), places_b]).astype(jnp.int32)
    received, weights, crossing, places_a, places_b = lax.optimization_barrier(
        (received, weights, crossing, places_a, places_b)
    )

    my_shards = lax.dynamic_index_in_dim(shard_lists, seq_index, 0, keepdims=False)
    my_places = lax.dynamic_index_in_dim(places, seq_index, 0, keepdims=False)
    row_index = (my_shards * capacity + my_places).reshape(NEIGH, N_Z, N_CORE, 2)
    row_index = row_index.transpose(2, 3, 1, 0)[:, ::-1]
    row_index = jnp.where(core == 0, row_index, row_index[::-1]).reshape(-1)
    count = row_index.shape[0] // 2
    mine, theirs = pick(received, row_index, jnp.zeros((), jnp.int32), piece, [count] * 2)
    mine, theirs = mine.reshape(-1, enc), theirs.reshape(-1, enc)

    def hop(value, steps, cross):
        pairs = [
            (z * N_CORE + c, (z + steps) % N_Z * N_CORE + (c + cross) % N_CORE)
            for z in range(N_Z)
            for c in range(N_CORE)
        ]
        return lax.ppermute(value, ("z", "core"), pairs)

    def add(*terms):
        return sum(term.astype(F32) for term in terms).astype(BF16)

    side = model // 2

    def total(here_left, here_right, up, down, up_left, down_right):
        left, right = add(here_left, down[:, :side], up_left), add(here_right, up[:, side:], down_right)
        return jnp.concatenate([left, right], axis=1)

    ring = [hop(mine, 1, 0), hop(theirs, -1, 1), hop(theirs, 1, 1), hop(mine, -1, 0)]
    swapped = hop(theirs, 0, 1)
    swapped, crossing = lax.optimization_barrier((swapped, crossing))
    crossing = lax.ppermute(crossing, ("seq", "core"), [(2 * i + 2, 2 * i + 1) for i in range(n_seq - 1)])
    near = project(weights[:4], (mine, swapped))
    ring, crossing, near = lax.optimization_barrier((ring, crossing, near))
    far = hop(ring[0], 1, 0), hop(ring[1], -1, 0)
    near = (*near, *project(weights[:4], ring))

    up_a, down_a, above_a, below_a, *rest = attend(
        0, places_a, second_queries, crossing, near, (*far, *weights[:4]), weights[4:]
    )
    here_a, far = rest[:2], rest[2:]
    up_a, down_a = step(up_a, "z", 1), step(down_a, "z", -1)
    up_b, down_b, above_b, below_b, *here_b = attend(1, places_b, first_queries, crossing, near, far, weights[4:])
    up_a, down_a, up_b, down_b = lax.optimization_barrier((up_a, down_a, up_b, down_b))
    above_a, below_a = lax.optimization_barrier((add(above_a, up_a[:, :side]), add(below_a, down_a[:, side:])))
    up_left_a, down_right_a = step(above_a, "z", 1), step(below_a, "z", -1)
    up_b, down_b = step(up_b, "z", 1), step(down_b, "z", -1)
    out_a = total(*here_a, up_a, down_a, up_left_a, down_right_a)

    pairs = []
    for i in range(0, n_seq * N_Z * N_CORE, 2):
        pairs.append((i, i + 1))
        if i % (N_Z * N_CORE):
            pairs.append((i + 1, i))
        elif i + N_Z * N_CORE < n_seq * N_Z * N_CORE:
            pairs.append((i + 1, i + N_Z * N_CORE))
    head = lax.ppermute(out_a, ("seq", "z", "core"), pairs)
    head, up_b, down_b = lax.optimization_barrier((head, up_b, down_b))
    above_b, below_b = lax.optimization_barrier((add(above_b, up_b[:, :side]), add(below_b, down_b[:, side:])))
    up_left_b, down_right_b = step(above_b, "z", 1), step(below_b, "z", -1)
    out_b = total(*here_b, up_b, down_b, up_left_b, down_right_b)
    return jnp.concatenate([head[1:], out_b, out_a[:1]], axis=0)


def solution(mesh):
    n_seq = mesh.devices.shape[0]
    fine = Mesh(mesh.devices.reshape(n_seq, N_Z, N_CORE), ("seq", "z", "core"))
    db = ("z", "core")
    return jax.shard_map(
        body,
        mesh=fine,
        in_specs=(
            P("seq", None),
            P(None, db),
            P(None, db),
            P(None, db),
            P(db, None),
            P("seq", None, None),
            P(),
            P(),
        ),
        out_specs=P(("seq", "z", "core"), None),
        check_vma=False,
    )
```

```python
import functools
import math

import jax
import jax.numpy as jnp
from jax import lax
from jax.experimental import pallas as pl
from jax.experimental.pallas import tpu as pltpu
from jax.sharding import Mesh, PartitionSpec as P

HS = 128
CL = 64
NB_LEN = 128
NEIGH = 2
N_Z = 4
N_CORE = 2
BLOCK = 128
F32 = jnp.float32
BF16 = jnp.bfloat16
SHARE = 0.4
LIMIT = 60 * 1024 * 1024
GRANT = 32 * 1024 * 1024


def step(value, axis, steps):
    count = lax.axis_size(axis)
    return lax.ppermute(value, axis, [(i, (i + steps) % count) for i in range(count)])


def cost(flops):
    return pl.CostEstimate(flops=int(flops * SHARE), bytes_accessed=int(flops * SHARE / 1000), transcendentals=0)


def dot(a, b):
    return jnp.dot(a, b, preferred_element_type=F32)


def bucket_places(shards):
    count = shards.shape[1]
    same_shard = shards[:, :, None] == shards[:, None, :]
    earlier = jnp.arange(count)[None, :] < jnp.arange(count)[:, None]
    return jnp.sum((same_shard & earlier[None]).astype(jnp.int32), axis=2)


def pick_kernel(index_ref, start_ref, source_ref, *refs):
    out_refs, rows_ref, sem = refs[:-2], refs[-2], refs[-1]
    rows = rows_ref.shape[1]
    start = pl.multiple_of(start_ref[0] * rows, rows)
    copy = pltpu.make_async_copy(source_ref.at[:, pl.ds(start, rows)], rows_ref, sem)
    copy.start()
    copy.wait()
    place = 0
    for out_ref in out_refs:
        for i in range(out_ref.shape[0]):
            out_ref[i] = rows_ref[index_ref[place]]
            place += 1


def pick(source, index, start, rows, counts, limit):
    shapes = [(count, rows, source.shape[2]) for count in counts]
    return pl.pallas_call(
        pick_kernel,
        grid_spec=pltpu.PrefetchScalarGridSpec(
            num_scalar_prefetch=2,
            grid=(1,),
            in_specs=[pl.BlockSpec(memory_space=pltpu.HBM)],
            out_specs=[pl.BlockSpec(shape, lambda i, index, start: (0, 0, 0)) for shape in shapes],
            scratch_shapes=[pltpu.VMEM((source.shape[0], rows, source.shape[2]), source.dtype), pltpu.SemaphoreType.DMA],
        ),
        out_shape=[jax.ShapeDtypeStruct(shape, source.dtype) for shape in shapes],
        cost_estimate=cost(1e9),
        compiler_params=pltpu.CompilerParams(vmem_limit_bytes=limit * 1024 * 1024),
    )(index, start.reshape(1), source)


def query_kernel(core_ref, x_hbm, wa_hbm, wb_hbm, first_ref, second_ref, crossing_ref, x_ref, wa_ref, wb_ref, sems):
    half = wa_ref.shape[1]
    copies = []
    for j in range(N_Z):
        block = N_CORE * j + core_ref[0]
        after = lax.rem(block + 1, N_Z * N_CORE)
        copies.append(pltpu.make_async_copy(x_hbm.at[block], x_ref.at[j, :BLOCK], sems.at[2 * j]))
        copies.append(pltpu.make_async_copy(x_hbm.at[after, :CL], x_ref.at[j, BLOCK:], sems.at[2 * j + 1]))
    copies.append(pltpu.make_async_copy(wa_hbm, wa_ref, sems.at[2 * N_Z]))
    copies.append(pltpu.make_async_copy(wb_hbm, wb_ref, sems.at[2 * N_Z + 1]))
    for copy in copies:
        copy.start()
    for j in range(N_Z):
        copies[2 * j].wait()
        copies[2 * j + 1].wait()
        source = x_ref[j].astype(F32)
        scale = lax.rsqrt(jnp.mean(source * source, axis=-1, keepdims=True) + 1e-05)
        x_ref[j] = (source * scale).astype(BF16)
    rows = BLOCK + CL
    for i, weight_ref in enumerate((wa_ref, wb_ref)):
        copies[2 * N_Z + i].wait()
        here, there = slice(i * half, (i + 1) * half), slice((1 - i) * half, (2 - i) * half)
        product = dot(x_ref[...].reshape(N_Z * rows, -1), weight_ref[...])
        for j in range(N_Z):
            rolled = pltpu.roll(product[j * rows : (j + 1) * rows], 1, 0).astype(BF16)
            first_ref[j, :, here] = rolled[CL:BLOCK]
            second_ref[j, :, here] = rolled[BLOCK:]
            if j == 0:
                crossing_ref[:, there] = rolled[:CL]


def project_queries(decoder, weight_a, weight_b, core):
    model, half = weight_a.shape
    blocks = decoder.reshape(N_Z * N_CORE, BLOCK, model)
    shape = (N_Z, CL, 2 * half)
    out_spec = pl.BlockSpec(shape, lambda i, core: (0, 0, 0))
    return pl.pallas_call(
        query_kernel,
        grid_spec=pltpu.PrefetchScalarGridSpec(
            num_scalar_prefetch=1,
            grid=(1,),
            in_specs=[pl.BlockSpec(memory_space=pltpu.HBM)] * 3,
            out_specs=[out_spec, out_spec, pl.BlockSpec(shape[1:], lambda i, core: (0, 0))],
            scratch_shapes=[
                pltpu.VMEM((N_Z, BLOCK + CL, model), BF16),
                pltpu.VMEM((model, half), BF16),
                pltpu.VMEM((model, half), BF16),
                pltpu.SemaphoreType.DMA((2 * N_Z + 2,)),
            ],
        ),
        out_shape=[jax.ShapeDtypeStruct(dims, BF16) for dims in (shape, shape, shape[1:])],
        cost_estimate=cost(3e9),
        compiler_params=pltpu.CompilerParams(vmem_limit_bytes=LIMIT),
    )(core.reshape(1), blocks, weight_a, weight_b)


def project_kernel(low_ref, high_ref, *refs):
    rows = jnp.concatenate([low_ref[...], high_ref[...]], axis=0)
    for weight_ref, out_ref in zip(refs[:4], refs[4:]):
        out_ref[...] = dot(rows, weight_ref[...]).astype(BF16).reshape(out_ref.shape)


def project(weights, parts):
    rows, enc = parts[0].shape
    width = weights[0].shape[1]
    shape = (len(parts), 2, N_Z, rows // (2 * N_Z), width)
    return pl.pallas_call(
        project_kernel,
        out_shape=[jax.ShapeDtypeStruct(shape, BF16)] * 4,
        cost_estimate=cost(2e9),
        compiler_params=pltpu.CompilerParams(vmem_limit_bytes=GRANT),
    )(*parts, *weights)


def span_kernel(group, place_ref, *refs):
    refs = list(refs)

    def take(count):
        taken = refs[:count]
        del refs[:count]
        return taken

    near_refs, row_refs, weight_refs = take(12), take(2), take(4)
    q_ref, crossing_ref = take(2)
    out_weight_refs, out_refs, far_kv_refs = take(2), take(6), take(4)
    count = row_refs[0].shape[0] // 2
    rows = jnp.concatenate([ref[group * count : (group + 1) * count] for ref in row_refs], axis=0)
    for weight_ref, far_kv_ref in zip(weight_refs, far_kv_refs):
        far_kv_ref[...] = dot(rows, weight_ref[...]).astype(BF16).reshape(far_kv_ref.shape)
    (context_ref,) = refs
    half, model = out_weight_refs[0].shape
    is_first_row = lax.broadcasted_iota(jnp.int32, (CL, HS), 0) == 0
    heads = [(side, lower) for side in (0, 1) for lower in range(0, half, HS)]

    def attend_span(span, carry):
        def columns(i, lower):
            parts = [near_refs[j][:, group, span, :, lower : lower + HS] for j in range(i, 12, 4)]
            parts.append(far_kv_refs[i][:, span, :, lower : lower + HS])
            return jnp.concatenate([part.reshape(-1, HS) for part in parts], axis=0)

        crosses = (span == N_Z - 1) & (place_ref[N_Z] == 1)
        scores = []
        for side, lower in heads:
            place = slice(side * half + lower, side * half + lower + HS)
            q = q_ref[span, :, place]
            if group == 0:
                q = jnp.where(is_first_row | jnp.logical_not(crosses), q, crossing_ref[:, place])
            k = columns(2 * side, lower)
            scores.append(lax.dot_general(q, k, (((1,), (1,)), ((), ())), preferred_element_type=F32))
        probs = []
        for score in scores:
            score = score * (1.0 / math.sqrt(HS))
            weights = jnp.exp(score - jnp.max(score, axis=-1, keepdims=True))
            total = jnp.sum(weights, axis=-1, keepdims=True)
            probs.append((weights * (1.0 / total)).astype(BF16))
        for (side, lower), prob in zip(heads, probs):
            v = columns(2 * side + 1, lower)
            context_ref[span, :, side * half + lower : side * half + lower + HS] = dot(prob, v).astype(BF16)
        return carry

    lax.fori_loop(0, N_Z, attend_span, 0)

    blocks = [context_ref[place_ref[i]] for i in range(N_Z)]
    if group == 0:
        is_first_row = lax.broadcasted_iota(jnp.int32, blocks[0].shape, 0) == 0
        blocks = [jnp.where(is_first_row, context_ref[place_ref[N_Z + 1 + i]], blocks[i]) for i in range(N_Z)]
    context = jnp.concatenate(blocks, axis=0)
    up, down, above, below, here_left, here_right = out_refs
    tile = model // 4
    for lower in range(0, model, tile):
        place = slice(lower, lower + tile)
        product = dot(context[:, :half], out_weight_refs[0][:, place])
        product = (product + dot(context[:, half:], out_weight_refs[1][:, place])).astype(BF16)
        blocks = [product[i * CL : (i + 1) * CL] for i in range(N_Z)]
        inner = slice(lower % (model // 2), lower % (model // 2) + tile)
        if lower < model // 2:
            up[:, place], down[:, place], above[:, inner], here_left[:, inner] = blocks[0], blocks[2], blocks[1], blocks[3]
        else:
            up[:, place], down[:, place], below[:, inner], here_right[:, inner] = blocks[1], blocks[0], blocks[2], blocks[3]


def attend(group, places, queries, crossing, near, far, weights):
    spans, tokens, width = queries.shape
    half, model = weights[4].shape
    outs = [(tokens, model)] * 2 + [(tokens, model // 2)] * 4
    scratch = [(2, spans, near[0].shape[3], half)] * 4 + [queries.shape]
    operands = (*near, *far, *weights[:4], queries, crossing, *weights[4:])
    vmem = pl.BlockSpec(memory_space=pltpu.VMEM)
    return pl.pallas_call(
        functools.partial(span_kernel, group),
        grid_spec=pltpu.PrefetchScalarGridSpec(
            num_scalar_prefetch=1,
            grid=(),
            in_specs=[vmem] * len(operands),
            out_specs=[vmem] * len(outs),
            scratch_shapes=[pltpu.VMEM(shape, BF16) for shape in scratch],
        ),
        out_shape=[jax.ShapeDtypeStruct(shape, BF16) for shape in outs],
        cost_estimate=cost(5e9),
        compiler_params=pltpu.CompilerParams(vmem_limit_bytes=GRANT),
    )(places, *operands)


def body(decoder, w_query, w_key, w_value, w_out, database, nb_shard, nb_slot):
    n_seq = lax.axis_size("seq")
    seq_index, z_index, core = lax.axis_index("seq"), lax.axis_index("z"), lax.axis_index("core")
    tok_rows, model = decoder.shape
    spans = tok_rows // CL
    requests = NEIGH * spans
    capacity = (requests + n_seq - 1) // n_seq + 1
    slots, _, enc = database.shape
    piece = NB_LEN // (N_Z * N_CORE)

    bits = (slots - 1).bit_length()
    lists = (nb_shard.T << bits) + nb_slot.T
    lists = lists.reshape(NEIGH, n_seq, spans).transpose(1, 0, 2).reshape(n_seq, requests)
    shard_lists, slot_lists = lists >> bits, lists & ((1 << bits) - 1)
    places = bucket_places(shard_lists)
    picked = (shard_lists == seq_index)[:, None, :] & (places[:, None, :] == jnp.arange(capacity)[None, :, None])
    send_slot = jnp.sum(jnp.where(picked, slot_lists[:, None, :], 0), axis=2)
    (outgoing,) = pick(database, send_slot.reshape(-1), z_index * N_CORE + core, piece, [n_seq * capacity], 60)
    received = lax.all_to_all(
        outgoing.reshape(n_seq, capacity, piece, enc), "seq", split_axis=0, concat_axis=0, tiled=True
    )
    received = received.reshape(n_seq * capacity, piece, enc)

    w_query_other = step(w_query, "core", 1)
    weights = (w_key, w_value, *(step(weight, "core", 1) for weight in (w_key, w_value)), w_out, step(w_out, "core", 1))
    first_queries, second_queries, crossing = project_queries(decoder, w_query, w_query_other, core)
    distance = jnp.array([2, 1, 3, 0], jnp.int32)
    places_b = (z_index + distance) % N_Z
    places_a = (z_index + distance + (N_Z - 1) * core) % N_Z
    places_a = jnp.concatenate([places_a, core.reshape(1), places_b]).astype(jnp.int32)
    received, weights, crossing, places_a, places_b = lax.optimization_barrier(
        (received, weights, crossing, places_a, places_b)
    )

    my_shards = lax.dynamic_index_in_dim(shard_lists, seq_index, 0, keepdims=False)
    my_places = lax.dynamic_index_in_dim(places, seq_index, 0, keepdims=False)
    row_index = (my_shards * capacity + my_places).reshape(NEIGH, N_Z, N_CORE, 2)
    row_index = row_index.transpose(2, 3, 1, 0)[:, ::-1]
    row_index = jnp.where(core == 0, row_index, row_index[::-1]).reshape(-1)
    count = row_index.shape[0] // 2
    mine, theirs = pick(received, row_index, jnp.zeros((), jnp.int32), piece, [count] * 2, 30)
    mine, theirs = mine.reshape(-1, enc), theirs.reshape(-1, enc)

    def hop(value, steps, cross):
        pairs = [
            (z * N_CORE + c, (z + steps) % N_Z * N_CORE + (c + cross) % N_CORE)
            for z in range(N_Z)
            for c in range(N_CORE)
        ]
        return lax.ppermute(value, ("z", "core"), pairs)

    def add(*terms):
        return sum(term.astype(F32) for term in terms).astype(BF16)

    side = model // 2

    def total(here_left, here_right, up, down, up_left, down_right):
        left, right = add(here_left, down[:, :side], up_left), add(here_right, up[:, side:], down_right)
        return jnp.concatenate([left, right], axis=1)

    ring = hop(mine, 1, 0), hop(theirs, -1, 1)
    swapped = hop(theirs, 0, 1)
    near = project(weights[:4], (mine, swapped))
    near, mine, theirs, crossing = lax.optimization_barrier((near, mine, theirs, crossing))
    ring_after = hop(theirs, 1, 1), hop(mine, -1, 0)
    crossing = lax.ppermute(crossing, ("seq", "core"), [(2 * i + 2, 2 * i + 1) for i in range(n_seq - 1)])
    far = hop(ring[0], 1, 0), hop(ring[1], -1, 0)
    near = (*near, *project(weights[:4], ring), *project(weights[:4], ring_after))

    up_a, down_a, above_a, below_a, *here_a = attend(0, places_a, second_queries, crossing, near, far, weights)
    up_a, down_a = step(up_a, "z", 1), step(down_a, "z", -1)
    up_b, down_b, above_b, below_b, *here_b = attend(1, places_b, first_queries, crossing, near, far, weights)
    up_a, down_a, up_b, down_b = lax.optimization_barrier((up_a, down_a, up_b, down_b))
    above_a, below_a = lax.optimization_barrier((add(above_a, up_a[:, :side]), add(below_a, down_a[:, side:])))
    up_left_a, down_right_a = step(above_a, "z", 1), step(below_a, "z", -1)
    up_b, down_b = step(up_b, "z", 1), step(down_b, "z", -1)
    out_a = total(*here_a, up_a, down_a, up_left_a, down_right_a)

    pairs = []
    for i in range(0, n_seq * N_Z * N_CORE, 2):
        pairs.append((i, i + 1))
        if i % (N_Z * N_CORE):
            pairs.append((i + 1, i))
        elif i + N_Z * N_CORE < n_seq * N_Z * N_CORE:
            pairs.append((i + 1, i + N_Z * N_CORE))
    head = lax.ppermute(out_a, ("seq", "z", "core"), pairs)
    head, up_b, down_b = lax.optimization_barrier((head, up_b, down_b))
    above_b, below_b = lax.optimization_barrier((add(above_b, up_b[:, :side]), add(below_b, down_b[:, side:])))
    up_left_b, down_right_b = step(above_b, "z", 1), step(below_b, "z", -1)
    out_b = total(*here_b, up_b, down_b, up_left_b, down_right_b)
    return jnp.concatenate([head[1:], out_b, out_a[:1]], axis=0)


def solution(mesh):
    n_seq = mesh.devices.shape[0]
    fine = Mesh(mesh.devices.reshape(n_seq, N_Z, N_CORE), ("seq", "z", "core"))
    db = ("z", "core")
    return jax.shard_map(
        body,
        mesh=fine,
        in_specs=(
            P("seq", None),
            P(None, db),
            P(None, db),
            P(None, db),
            P(db, None),
            P("seq", None, None),
            P(),
            P(),
        ),
        out_specs=P(("seq", "z", "core"), None),
        check_vma=False,
    )
```

```python
import functools
import math

import jax
import jax.numpy as jnp
from jax import lax
from jax.experimental import pallas as pl
from jax.experimental.pallas import tpu as pltpu
from jax.sharding import Mesh, PartitionSpec as P

HS = 128
CL = 64
NB_LEN = 128
NEIGH = 2
N_Z = 4
N_CORE = 2
BLOCK = 128
F32 = jnp.float32
BF16 = jnp.bfloat16
SHARE = 0.4
LIMIT = 60 * 1024 * 1024
GRANT = 32 * 1024 * 1024


def step(value, axis, steps):
    count = lax.axis_size(axis)
    return lax.ppermute(value, axis, [(i, (i + steps) % count) for i in range(count)])


def cost(flops):
    return pl.CostEstimate(flops=int(flops * SHARE), bytes_accessed=int(flops * SHARE / 1000), transcendentals=0)


def dot(a, b):
    return jnp.dot(a, b, preferred_element_type=F32)


def bucket_places(shards):
    count = shards.shape[1]
    same_shard = shards[:, :, None] == shards[:, None, :]
    earlier = jnp.arange(count)[None, :] < jnp.arange(count)[:, None]
    return jnp.sum((same_shard & earlier[None]).astype(jnp.int32), axis=2)


def pick_kernel(index_ref, start_ref, source_ref, *refs):
    out_refs, rows_ref, sem = refs[:-2], refs[-2], refs[-1]
    rows = rows_ref.shape[1]
    start = pl.multiple_of(start_ref[0] * rows, rows)
    copy = pltpu.make_async_copy(source_ref.at[:, pl.ds(start, rows)], rows_ref, sem)
    copy.start()
    copy.wait()
    place = 0
    for out_ref in out_refs:
        for i in range(out_ref.shape[0]):
            out_ref[i] = rows_ref[index_ref[place]]
            place += 1


def pick(source, index, start, rows, counts, limit):
    shapes = [(count, rows, source.shape[2]) for count in counts]
    return pl.pallas_call(
        pick_kernel,
        grid_spec=pltpu.PrefetchScalarGridSpec(
            num_scalar_prefetch=2,
            grid=(1,),
            in_specs=[pl.BlockSpec(memory_space=pltpu.HBM)],
            out_specs=[pl.BlockSpec(shape, lambda i, index, start: (0, 0, 0)) for shape in shapes],
            scratch_shapes=[pltpu.VMEM((source.shape[0], rows, source.shape[2]), source.dtype), pltpu.SemaphoreType.DMA],
        ),
        out_shape=[jax.ShapeDtypeStruct(shape, source.dtype) for shape in shapes],
        cost_estimate=cost(1e9),
        compiler_params=pltpu.CompilerParams(vmem_limit_bytes=limit * 1024 * 1024),
    )(index, start.reshape(1), source)


def query_kernel(core_ref, x_hbm, wa_hbm, wb_hbm, first_ref, second_ref, crossing_ref, x_ref, wa_ref, wb_ref, sems):
    half = wa_ref.shape[1]
    copies = []
    for j in range(N_Z):
        block = N_CORE * j + core_ref[0]
        after = lax.rem(block + 1, N_Z * N_CORE)
        copies.append(pltpu.make_async_copy(x_hbm.at[block], x_ref.at[j, :BLOCK], sems.at[2 * j]))
        copies.append(pltpu.make_async_copy(x_hbm.at[after, :CL], x_ref.at[j, BLOCK:], sems.at[2 * j + 1]))
    copies.append(pltpu.make_async_copy(wa_hbm, wa_ref, sems.at[2 * N_Z]))
    copies.append(pltpu.make_async_copy(wb_hbm, wb_ref, sems.at[2 * N_Z + 1]))
    for copy in copies:
        copy.start()
    for j in range(N_Z):
        copies[2 * j].wait()
        copies[2 * j + 1].wait()
        source = x_ref[j].astype(F32)
        scale = lax.rsqrt(jnp.mean(source * source, axis=-1, keepdims=True) + 1e-05)
        x_ref[j] = (source * scale).astype(BF16)
    rows = BLOCK + CL
    for i, weight_ref in enumerate((wa_ref, wb_ref)):
        copies[2 * N_Z + i].wait()
        here, there = slice(i * half, (i + 1) * half), slice((1 - i) * half, (2 - i) * half)
        product = dot(x_ref[...].reshape(N_Z * rows, -1), weight_ref[...])
        for j in range(N_Z):
            rolled = pltpu.roll(product[j * rows : (j + 1) * rows], 1, 0).astype(BF16)
            first_ref[j, :, here] = rolled[CL:BLOCK]
            second_ref[j, :, here] = rolled[BLOCK:]
            if j == 0:
                crossing_ref[:, there] = rolled[:CL]


def project_queries(decoder, weight_a, weight_b, core):
    model, half = weight_a.shape
    blocks = decoder.reshape(N_Z * N_CORE, BLOCK, model)
    shape = (N_Z, CL, 2 * half)
    out_spec = pl.BlockSpec(shape, lambda i, core: (0, 0, 0))
    return pl.pallas_call(
        query_kernel,
        grid_spec=pltpu.PrefetchScalarGridSpec(
            num_scalar_prefetch=1,
            grid=(1,),
            in_specs=[pl.BlockSpec(memory_space=pltpu.HBM)] * 3,
            out_specs=[out_spec, out_spec, pl.BlockSpec(shape[1:], lambda i, core: (0, 0))],
            scratch_shapes=[
                pltpu.VMEM((N_Z, BLOCK + CL, model), BF16),
                pltpu.VMEM((model, half), BF16),
                pltpu.VMEM((model, half), BF16),
                pltpu.SemaphoreType.DMA((2 * N_Z + 2,)),
            ],
        ),
        out_shape=[jax.ShapeDtypeStruct(dims, BF16) for dims in (shape, shape, shape[1:])],
        cost_estimate=cost(3e9),
        compiler_params=pltpu.CompilerParams(vmem_limit_bytes=LIMIT),
    )(core.reshape(1), blocks, weight_a, weight_b)


def project_kernel(count, *refs):
    low_ref, high_ref, weight_refs, carried_hbm = refs[0], refs[1], refs[2:6], refs[6 : 6 + count]
    out_refs, carried_refs = refs[6 + count : 10 + count], refs[10 + count : 10 + 2 * count]
    copies = [pltpu.make_async_copy(carried_hbm[i], carried_refs[i], refs[-1].at[i]) for i in range(count)]
    for copy in copies:
        copy.start()
    rows = jnp.concatenate([low_ref[...], high_ref[...]], axis=0)
    for weight_ref, out_ref in zip(weight_refs, out_refs):
        out_ref[...] = dot(rows, weight_ref[...]).astype(BF16).reshape(out_ref.shape)
    for copy in copies:
        copy.wait()


def project(weights, parts, carried=()):
    rows, enc = parts[0].shape
    width = weights[0].shape[1]
    shape = (len(parts), 2, N_Z, rows // (2 * N_Z), width)
    vmem = pl.BlockSpec(memory_space=pltpu.VMEM)
    return pl.pallas_call(
        functools.partial(project_kernel, len(carried)),
        in_specs=[vmem] * 6 + [pl.BlockSpec(memory_space=pltpu.HBM)] * len(carried),
        out_specs=[vmem] * (4 + len(carried)),
        out_shape=[jax.ShapeDtypeStruct(shape, BF16)] * 4
        + [jax.ShapeDtypeStruct(value.shape, value.dtype) for value in carried],
        scratch_shapes=[pltpu.SemaphoreType.DMA((max(1, len(carried)),))],
        cost_estimate=cost(2e9),
        compiler_params=pltpu.CompilerParams(vmem_limit_bytes=GRANT),
    )(*parts, *weights, *carried)


def span_kernel(group, place_ref, *refs):
    refs = list(refs)

    def take(count):
        taken = refs[:count]
        del refs[:count]
        return taken

    near_refs, row_refs, weight_refs = take(12), take(2), take(4)
    q_ref, crossing_ref = take(2)
    out_weight_refs, out_refs, far_kv_refs = take(2), take(6 if group == 0 else 8), take(4)
    count = row_refs[0].shape[0] // 2
    rows = jnp.concatenate([ref[group * count : (group + 1) * count] for ref in row_refs], axis=0)
    for weight_ref, far_kv_ref in zip(weight_refs, far_kv_refs):
        far_kv_ref[...] = dot(rows, weight_ref[...]).astype(BF16).reshape(far_kv_ref.shape)
    (context_ref,) = refs
    half, model = out_weight_refs[0].shape
    is_first_row = lax.broadcasted_iota(jnp.int32, (CL, HS), 0) == 0
    heads = [(side, lower) for side in (0, 1) for lower in range(0, half, HS)]

    def attend_span(span, carry):
        def columns(i, lower):
            parts = [near_refs[j][:, group, span, :, lower : lower + HS] for j in range(i, 12, 4)]
            parts.append(far_kv_refs[i][:, span, :, lower : lower + HS])
            return jnp.concatenate([part.reshape(-1, HS) for part in parts], axis=0)

        crosses = (span == N_Z - 1) & (place_ref[N_Z] == 1)
        scores = []
        for side, lower in heads:
            place = slice(side * half + lower, side * half + lower + HS)
            q = q_ref[span, :, place]
            if group == 0:
                q = jnp.where(is_first_row | jnp.logical_not(crosses), q, crossing_ref[:, place])
            k = columns(2 * side, lower)
            scores.append(lax.dot_general(q, k, (((1,), (1,)), ((), ())), preferred_element_type=F32))
        probs = []
        for score in scores:
            score = score * (1.0 / math.sqrt(HS))
            weights = jnp.exp(score - jnp.max(score, axis=-1, keepdims=True))
            total = jnp.sum(weights, axis=-1, keepdims=True)
            probs.append((weights * (1.0 / total)).astype(BF16))
        for (side, lower), prob in zip(heads, probs):
            v = columns(2 * side + 1, lower)
            context_ref[span, :, side * half + lower : side * half + lower + HS] = dot(prob, v).astype(BF16)
        return carry

    lax.fori_loop(0, N_Z, attend_span, 0, unroll=N_Z)

    blocks = [context_ref[place_ref[i]] for i in range(N_Z)]
    if group == 0:
        is_first_row = lax.broadcasted_iota(jnp.int32, blocks[0].shape, 0) == 0
        blocks = [jnp.where(is_first_row, context_ref[place_ref[N_Z + 1 + i]], blocks[i]) for i in range(N_Z)]
    context = jnp.concatenate(blocks, axis=0)
    tile = model // 4
    for lower in range(0, model, tile):
        place = slice(lower, lower + tile)
        product = dot(context[:, :half], out_weight_refs[0][:, place])
        product = (product + dot(context[:, half:], out_weight_refs[1][:, place])).astype(BF16)
        side, start = lower // (model // 2), lower % (model // 2)
        for i in range(N_Z):
            block = product[i * CL : (i + 1) * CL]
            if group == 1:
                out_refs[2 * i + side][:, start : start + tile] = block
            elif i < N_Z - 1 and (i, side) not in ((1, 0), (2, 1)):
                out_refs[(0, 0, 1)[i] if i != 0 else side][:, place] = block
            else:
                out_refs[{(1, 0): 2, (2, 1): 3, (3, 0): 4, (3, 1): 5}[i, side]][:, start : start + tile] = block


def attend(group, places, queries, crossing, near, far, weights):
    spans, tokens, width = queries.shape
    half, model = weights[4].shape
    outs = [(tokens, model)] * 2 + [(tokens, model // 2)] * 4 if group == 0 else [(tokens, model // 2)] * 8
    scratch = [(2, spans, near[0].shape[3], half)] * 4 + [queries.shape]
    operands = (*near, *far, *weights[:4], queries, crossing, *weights[4:])
    vmem = pl.BlockSpec(memory_space=pltpu.VMEM)
    return pl.pallas_call(
        functools.partial(span_kernel, group),
        grid_spec=pltpu.PrefetchScalarGridSpec(
            num_scalar_prefetch=1,
            grid=(),
            in_specs=[vmem] * len(operands),
            out_specs=[vmem] * len(outs),
            scratch_shapes=[pltpu.VMEM(shape, BF16) for shape in scratch],
        ),
        out_shape=[jax.ShapeDtypeStruct(shape, BF16) for shape in outs],
        cost_estimate=cost(5e9),
        compiler_params=pltpu.CompilerParams(vmem_limit_bytes=GRANT),
    )(places, *operands)


def body(decoder, w_query, w_key, w_value, w_out, database, nb_shard, nb_slot):
    n_seq = lax.axis_size("seq")
    seq_index, z_index, core = lax.axis_index("seq"), lax.axis_index("z"), lax.axis_index("core")
    tok_rows, model = decoder.shape
    spans = tok_rows // CL
    requests = NEIGH * spans
    capacity = (requests + n_seq - 1) // n_seq + 1
    slots, _, enc = database.shape
    piece = NB_LEN // (N_Z * N_CORE)

    bits = (slots - 1).bit_length()
    lists = (nb_shard.T << bits) + nb_slot.T
    lists = lists.reshape(NEIGH, n_seq, spans).transpose(1, 0, 2).reshape(n_seq, requests)
    shard_lists, slot_lists = lists >> bits, lists & ((1 << bits) - 1)
    places = bucket_places(shard_lists)
    picked = (shard_lists == seq_index)[:, None, :] & (places[:, None, :] == jnp.arange(capacity)[None, :, None])
    send_slot = jnp.sum(jnp.where(picked, slot_lists[:, None, :], 0), axis=2)
    (outgoing,) = pick(database, send_slot.reshape(-1), z_index * N_CORE + core, piece, [n_seq * capacity], 60)
    received = lax.all_to_all(
        outgoing.reshape(n_seq, capacity, piece, enc), "seq", split_axis=0, concat_axis=0, tiled=True
    )
    received = received.reshape(n_seq * capacity, piece, enc)

    w_query_other = step(w_query, "core", 1)
    weights = (w_key, w_value, *(step(weight, "core", 1) for weight in (w_key, w_value)), w_out, step(w_out, "core", 1))
    first_queries, second_queries, crossing = project_queries(decoder, w_query, w_query_other, core)
    distance = jnp.array([2, 1, 3, 0], jnp.int32)
    places_b = (z_index + distance) % N_Z
    places_a = (z_index + distance + (N_Z - 1) * core) % N_Z
    places_a = jnp.concatenate([places_a, core.reshape(1), places_b]).astype(jnp.int32)
    received, weights, crossing, places_a, places_b = lax.optimization_barrier(
        (received, weights, crossing, places_a, places_b)
    )

    my_shards = lax.dynamic_index_in_dim(shard_lists, seq_index, 0, keepdims=False)
    my_places = lax.dynamic_index_in_dim(places, seq_index, 0, keepdims=False)
    row_index = (my_shards * capacity + my_places).reshape(NEIGH, N_Z, N_CORE, 2)
    row_index = row_index.transpose(2, 3, 1, 0)[:, ::-1]
    row_index = jnp.where(core == 0, row_index, row_index[::-1]).reshape(-1)
    count = row_index.shape[0] // 2
    mine, theirs = pick(received, row_index, jnp.zeros((), jnp.int32), piece, [count] * 2, 30)
    mine, theirs = mine.reshape(-1, enc), theirs.reshape(-1, enc)

    def hop(value, steps, cross):
        pairs = [
            (z * N_CORE + c, (z + steps) % N_Z * N_CORE + (c + cross) % N_CORE)
            for z in range(N_Z)
            for c in range(N_CORE)
        ]
        return lax.ppermute(value, ("z", "core"), pairs)

    def add(*terms):
        return sum(term.astype(F32) for term in terms).astype(BF16)

    side = model // 2

    def total(here_left, here_right, down_left, up_right, up_left, down_right):
        left, right = add(here_left, down_left, up_left), add(here_right, up_right, down_right)
        return jnp.concatenate([left, right], axis=1)

    ring = hop(mine, 1, 0), hop(theirs, -1, 1)
    swapped = hop(theirs, 0, 1)
    *near, w_value_other, w_out_other = project(weights[:4], (mine, swapped), (weights[3], weights[5]))
    weights = (*weights[:3], w_value_other, weights[4], w_out_other)
    near, mine, theirs, crossing = lax.optimization_barrier((near, mine, theirs, crossing))
    ring_after = hop(theirs, 1, 1), hop(mine, -1, 0)
    crossing = lax.ppermute(crossing, ("seq", "core"), [(2 * i + 2, 2 * i + 1) for i in range(n_seq - 1)])
    far = hop(ring[0], 1, 0), hop(ring[1], -1, 0)
    near = (*near, *project(weights[:4], ring), *project(weights[:4], ring_after))

    up_a, down_a, above_a, below_a, *here_a = attend(0, places_a, second_queries, crossing, near, far, weights)
    up_a, down_a = step(up_a, "z", 1), step(down_a, "z", -1)
    sums_b = attend(1, places_b, first_queries, crossing, near, far, weights)
    up_a, down_a, sums_b = lax.optimization_barrier((up_a, down_a, sums_b))
    above_a, below_a = lax.optimization_barrier((add(above_a, up_a[:, :side]), add(below_a, down_a[:, side:])))
    up_left_a, down_right_a = step(above_a, "z", 1), step(below_a, "z", -1)
    up_b, down_b = step(sums_b[0], "z", 1), step(sums_b[1], "z", -1)
    up_right_b, down_left_b = step(sums_b[3], "z", 1), step(sums_b[4], "z", -1)
    out_a = total(*here_a, down_a[:, :side], up_a[:, side:], up_left_a, down_right_a)

    pairs = []
    for i in range(0, n_seq * N_Z * N_CORE, 2):
        pairs.append((i, i + 1))
        if i % (N_Z * N_CORE):
            pairs.append((i + 1, i))
        elif i + N_Z * N_CORE < n_seq * N_Z * N_CORE:
            pairs.append((i + 1, i + N_Z * N_CORE))
    head = lax.ppermute(out_a, ("seq", "z", "core"), pairs)
    above_b, below_b = lax.optimization_barrier((add(sums_b[2], up_b), add(sums_b[5], down_b)))
    up_left_b, down_right_b = step(above_b, "z", 1), step(below_b, "z", -1)
    out_b = total(*sums_b[6:], down_left_b, up_right_b, up_left_b, down_right_b)
    return jnp.concatenate([head[1:], out_b, out_a[:1]], axis=0)


def solution(mesh):
    n_seq = mesh.devices.shape[0]
    fine = Mesh(mesh.devices.reshape(n_seq, N_Z, N_CORE), ("seq", "z", "core"))
    db = ("z", "core")
    return jax.shard_map(
        body,
        mesh=fine,
        in_specs=(
            P("seq", None),
            P(None, db),
            P(None, db),
            P(None, db),
            P(db, None),
            P("seq", None, None),
            P(),
            P(),
        ),
        out_specs=P(("seq", "z", "core"), None),
        check_vma=False,
    )
```

```python
import functools
import math

import jax
import jax.numpy as jnp
from jax import lax
from jax.experimental import pallas as pl
from jax.experimental.pallas import tpu as pltpu
from jax.sharding import Mesh, PartitionSpec as P

HS = 128
CL = 64
NB_LEN = 128
NEIGH = 2
N_Z = 4
N_CORE = 2
BLOCK = 128
F32 = jnp.float32
BF16 = jnp.bfloat16
SHARE = 0.4
LIMIT = 60 * 1024 * 1024
GRANT = 32 * 1024 * 1024


def step(value, axis, steps):
    count = lax.axis_size(axis)
    return lax.ppermute(value, axis, [(i, (i + steps) % count) for i in range(count)])


def cost(flops):
    return pl.CostEstimate(flops=int(flops * SHARE), bytes_accessed=int(flops * SHARE / 1000), transcendentals=0)


def dot(a, b):
    return jnp.dot(a, b, preferred_element_type=F32)


def bucket_places(shards):
    count = shards.shape[1]
    same_shard = shards[:, :, None] == shards[:, None, :]
    earlier = jnp.arange(count)[None, :] < jnp.arange(count)[:, None]
    return jnp.sum((same_shard & earlier[None]).astype(jnp.int32), axis=2)


def pick_kernel(index_ref, start_ref, source_ref, *refs):
    out_refs, rows_ref, sem = refs[:-2], refs[-2], refs[-1]
    rows = rows_ref.shape[1]
    start = pl.multiple_of(start_ref[0] * rows, rows)
    copy = pltpu.make_async_copy(source_ref.at[:, pl.ds(start, rows)], rows_ref, sem)
    copy.start()
    copy.wait()
    place = 0
    for out_ref in out_refs:
        for i in range(out_ref.shape[0]):
            out_ref[i] = rows_ref[index_ref[place]]
            place += 1


def pick(source, index, start, rows, counts, limit):
    shapes = [(count, rows, source.shape[2]) for count in counts]
    return pl.pallas_call(
        pick_kernel,
        grid_spec=pltpu.PrefetchScalarGridSpec(
            num_scalar_prefetch=2,
            grid=(1,),
            in_specs=[pl.BlockSpec(memory_space=pltpu.HBM)],
            out_specs=[pl.BlockSpec(shape, lambda i, index, start: (0, 0, 0)) for shape in shapes],
            scratch_shapes=[pltpu.VMEM((source.shape[0], rows, source.shape[2]), source.dtype), pltpu.SemaphoreType.DMA],
        ),
        out_shape=[jax.ShapeDtypeStruct(shape, source.dtype) for shape in shapes],
        cost_estimate=cost(1e9),
        compiler_params=pltpu.CompilerParams(vmem_limit_bytes=limit * 1024 * 1024),
    )(index, start.reshape(1), source)


def query_kernel(core_ref, x_hbm, wa_hbm, wb_hbm, first_ref, second_ref, crossing_ref, x_ref, wa_ref, wb_ref, sems):
    half = wa_ref.shape[1]
    copies = []
    for j in range(N_Z):
        block = N_CORE * j + core_ref[0]
        after = lax.rem(block + 1, N_Z * N_CORE)
        copies.append(pltpu.make_async_copy(x_hbm.at[block], x_ref.at[j, :BLOCK], sems.at[2 * j]))
        copies.append(pltpu.make_async_copy(x_hbm.at[after, :CL], x_ref.at[j, BLOCK:], sems.at[2 * j + 1]))
    copies.append(pltpu.make_async_copy(wa_hbm, wa_ref, sems.at[2 * N_Z]))
    copies.append(pltpu.make_async_copy(wb_hbm, wb_ref, sems.at[2 * N_Z + 1]))
    for copy in copies:
        copy.start()
    for j in range(N_Z):
        copies[2 * j].wait()
        copies[2 * j + 1].wait()
        source = x_ref[j].astype(F32)
        scale = lax.rsqrt(jnp.mean(source * source, axis=-1, keepdims=True) + 1e-05)
        x_ref[j] = (source * scale).astype(BF16)
    rows = BLOCK + CL
    for i, weight_ref in enumerate((wa_ref, wb_ref)):
        copies[2 * N_Z + i].wait()
        here, there = slice(i * half, (i + 1) * half), slice((1 - i) * half, (2 - i) * half)
        product = dot(x_ref[...].reshape(N_Z * rows, -1), weight_ref[...])
        for j in range(N_Z):
            rolled = pltpu.roll(product[j * rows : (j + 1) * rows], 1, 0).astype(BF16)
            first_ref[j, :, here] = rolled[CL:BLOCK]
            second_ref[j, :, here] = rolled[BLOCK:]
            if j == 0:
                crossing_ref[:, there] = rolled[:CL]


def project_queries(decoder, weight_a, weight_b, core):
    model, half = weight_a.shape
    blocks = decoder.reshape(N_Z * N_CORE, BLOCK, model)
    shape = (N_Z, CL, 2 * half)
    out_spec = pl.BlockSpec(shape, lambda i, core: (0, 0, 0))
    return pl.pallas_call(
        query_kernel,
        grid_spec=pltpu.PrefetchScalarGridSpec(
            num_scalar_prefetch=1,
            grid=(1,),
            in_specs=[pl.BlockSpec(memory_space=pltpu.HBM)] * 3,
            out_specs=[out_spec, out_spec, pl.BlockSpec(shape[1:], lambda i, core: (0, 0))],
            scratch_shapes=[
                pltpu.VMEM((N_Z, BLOCK + CL, model), BF16),
                pltpu.VMEM((model, half), BF16),
                pltpu.VMEM((model, half), BF16),
                pltpu.SemaphoreType.DMA((2 * N_Z + 2,)),
            ],
        ),
        out_shape=[jax.ShapeDtypeStruct(dims, BF16) for dims in (shape, shape, shape[1:])],
        cost_estimate=cost(3e9),
        compiler_params=pltpu.CompilerParams(vmem_limit_bytes=LIMIT),
    )(core.reshape(1), blocks, weight_a, weight_b)


def project_kernel(count, *refs):
    low_ref, high_ref, weight_refs, carried_hbm = refs[0], refs[1], refs[2:6], refs[6 : 6 + count]
    out_refs, carried_refs = refs[6 + count : 10 + count], refs[10 + count : 10 + 2 * count]
    copies = [pltpu.make_async_copy(carried_hbm[i], carried_refs[i], refs[-1].at[i]) for i in range(count)]
    for copy in copies:
        copy.start()
    rows = jnp.concatenate([low_ref[...], high_ref[...]], axis=0)
    for weight_ref, out_ref in zip(weight_refs, out_refs):
        out_ref[...] = dot(rows, weight_ref[...]).astype(BF16).reshape(out_ref.shape)
    for copy in copies:
        copy.wait()


def project(weights, parts, carried=()):
    rows, enc = parts[0].shape
    width = weights[0].shape[1]
    shape = (len(parts), 2, N_Z, rows // (2 * N_Z), width)
    vmem = pl.BlockSpec(memory_space=pltpu.VMEM)
    return pl.pallas_call(
        functools.partial(project_kernel, len(carried)),
        in_specs=[vmem] * 6 + [pl.BlockSpec(memory_space=pltpu.HBM)] * len(carried),
        out_specs=[vmem] * (4 + len(carried)),
        out_shape=[jax.ShapeDtypeStruct(shape, BF16)] * 4
        + [jax.ShapeDtypeStruct(value.shape, value.dtype) for value in carried],
        scratch_shapes=[pltpu.SemaphoreType.DMA((max(1, len(carried)),))],
        cost_estimate=cost(2e9),
        compiler_params=pltpu.CompilerParams(vmem_limit_bytes=GRANT),
    )(*parts, *weights, *carried)


def span_kernel(group, place_ref, *refs):
    refs = list(refs)

    def take(count):
        taken = refs[:count]
        del refs[:count]
        return taken

    near_refs, row_refs, weight_refs = take(12), take(2), take(4)
    q_ref, crossing_ref = take(2)
    out_weight_refs, out_refs, far_kv_refs = take(2), take(6 if group == 0 else 8), take(4)
    rows = jnp.concatenate([ref[...] for ref in row_refs], axis=0)
    for weight_ref, far_kv_ref in zip(weight_refs, far_kv_refs):
        far_kv_ref[...] = dot(rows, weight_ref[...]).astype(BF16).reshape(far_kv_ref.shape)
    (context_ref,) = refs
    half, model = out_weight_refs[0].shape
    is_first_row = lax.broadcasted_iota(jnp.int32, (CL, HS), 0) == 0
    heads = [(side, lower) for side in (0, 1) for lower in range(0, half, HS)]

    def attend_span(span, carry):
        def columns(i, lower):
            parts = [near_refs[j][:, group, span, :, lower : lower + HS] for j in range(i, 12, 4)]
            parts.append(far_kv_refs[i][:, span, :, lower : lower + HS])
            return jnp.concatenate([part.reshape(-1, HS) for part in parts], axis=0)

        crosses = (span == N_Z - 1) & (place_ref[N_Z] == 1)
        scores = []
        for side, lower in heads:
            place = slice(side * half + lower, side * half + lower + HS)
            q = q_ref[span, :, place]
            if group == 0:
                q = jnp.where(is_first_row | jnp.logical_not(crosses), q, crossing_ref[:, place])
            k = columns(2 * side, lower)
            scores.append(lax.dot_general(q, k, (((1,), (1,)), ((), ())), preferred_element_type=F32))
        probs = []
        for score in scores:
            score = score * (1.0 / math.sqrt(HS))
            weights = jnp.exp(score - jnp.max(score, axis=-1, keepdims=True))
            total = jnp.sum(weights, axis=-1, keepdims=True)
            probs.append((weights * (1.0 / total)).astype(BF16))
        for (side, lower), prob in zip(heads, probs):
            v = columns(2 * side + 1, lower)
            context_ref[span, :, side * half + lower : side * half + lower + HS] = dot(prob, v).astype(BF16)
        return carry

    lax.fori_loop(0, N_Z, attend_span, 0, unroll=N_Z)

    blocks = [context_ref[place_ref[i]] for i in range(N_Z)]
    if group == 0:
        is_first_row = lax.broadcasted_iota(jnp.int32, blocks[0].shape, 0) == 0
        blocks = [jnp.where(is_first_row, context_ref[place_ref[N_Z + 1 + i]], blocks[i]) for i in range(N_Z)]
    context = jnp.concatenate(blocks, axis=0)
    tile = model // 4
    for lower in range(0, model, tile):
        place = slice(lower, lower + tile)
        product = dot(context[:, :half], out_weight_refs[0][:, place])
        product = (product + dot(context[:, half:], out_weight_refs[1][:, place])).astype(BF16)
        side, start = lower // (model // 2), lower % (model // 2)
        for i in range(N_Z):
            block = product[i * CL : (i + 1) * CL]
            if group == 1:
                out_refs[2 * i + side][:, start : start + tile] = block
            elif i < N_Z - 1 and (i, side) not in ((1, 0), (2, 1)):
                out_refs[(0, 0, 1)[i] if i != 0 else side][:, place] = block
            else:
                out_refs[{(1, 0): 2, (2, 1): 3, (3, 0): 4, (3, 1): 5}[i, side]][:, start : start + tile] = block


def attend(group, places, queries, crossing, near, far, weights):
    spans, tokens, width = queries.shape
    half, model = weights[4].shape
    outs = [(tokens, model)] * 2 + [(tokens, model // 2)] * 4 if group == 0 else [(tokens, model // 2)] * 8
    scratch = [(2, spans, near[0].shape[3], half)] * 4 + [queries.shape]
    operands = (*near, *far, *weights[:4], queries, crossing, *weights[4:])
    vmem = pl.BlockSpec(memory_space=pltpu.VMEM)
    return pl.pallas_call(
        functools.partial(span_kernel, group),
        grid_spec=pltpu.PrefetchScalarGridSpec(
            num_scalar_prefetch=1,
            grid=(),
            in_specs=[vmem] * len(operands),
            out_specs=[vmem] * len(outs),
            scratch_shapes=[pltpu.VMEM(shape, BF16) for shape in scratch],
        ),
        out_shape=[jax.ShapeDtypeStruct(shape, BF16) for shape in outs],
        cost_estimate=cost(5e9),
        compiler_params=pltpu.CompilerParams(vmem_limit_bytes=GRANT),
    )(places, *operands)


def body(decoder, w_query, w_key, w_value, w_out, database, nb_shard, nb_slot):
    n_seq = lax.axis_size("seq")
    seq_index, z_index, core = lax.axis_index("seq"), lax.axis_index("z"), lax.axis_index("core")
    tok_rows, model = decoder.shape
    spans = tok_rows // CL
    requests = NEIGH * spans
    capacity = (requests + n_seq - 1) // n_seq + 1
    slots, _, enc = database.shape
    piece = NB_LEN // (N_Z * N_CORE)

    bits = (slots - 1).bit_length()
    lists = (nb_shard.T << bits) + nb_slot.T
    lists = lists.reshape(NEIGH, n_seq, spans).transpose(1, 0, 2).reshape(n_seq, requests)
    shard_lists, slot_lists = lists >> bits, lists & ((1 << bits) - 1)
    places = bucket_places(shard_lists)
    picked = (shard_lists == seq_index)[:, None, :] & (places[:, None, :] == jnp.arange(capacity)[None, :, None])
    send_slot = jnp.sum(jnp.where(picked, slot_lists[:, None, :], 0), axis=2)
    (outgoing,) = pick(database, send_slot.reshape(-1), z_index * N_CORE + core, piece, [n_seq * capacity], 60)
    received = lax.all_to_all(
        outgoing.reshape(n_seq, capacity, piece, enc), "seq", split_axis=0, concat_axis=0, tiled=True
    )
    received = received.reshape(n_seq * capacity, piece, enc)

    w_query_other = step(w_query, "core", 1)
    weights = (w_key, w_value, *(step(weight, "core", 1) for weight in (w_key, w_value)), w_out, step(w_out, "core", 1))
    first_queries, second_queries, crossing = project_queries(decoder, w_query, w_query_other, core)
    distance = jnp.array([2, 1, 3, 0], jnp.int32)
    places_b = (z_index + distance) % N_Z
    places_a = (z_index + distance + (N_Z - 1) * core) % N_Z
    places_a = jnp.concatenate([places_a, core.reshape(1), places_b]).astype(jnp.int32)
    received, weights, crossing, places_a, places_b = lax.optimization_barrier(
        (received, weights, crossing, places_a, places_b)
    )

    my_shards = lax.dynamic_index_in_dim(shard_lists, seq_index, 0, keepdims=False)
    my_places = lax.dynamic_index_in_dim(places, seq_index, 0, keepdims=False)
    row_index = (my_shards * capacity + my_places).reshape(NEIGH, N_Z, N_CORE, 2)
    row_index = row_index.transpose(2, 3, 1, 0)[:, ::-1]
    row_index = jnp.where(core == 0, row_index, row_index[::-1]).reshape(-1)
    count = row_index.shape[0] // 2
    mine, theirs = pick(received, row_index, jnp.zeros((), jnp.int32), piece, [count] * 2, 30)
    mine, theirs = mine.reshape(-1, enc), theirs.reshape(-1, enc)

    def hop(value, steps, cross):
        pairs = [
            (z * N_CORE + c, (z + steps) % N_Z * N_CORE + (c + cross) % N_CORE)
            for z in range(N_Z)
            for c in range(N_CORE)
        ]
        return lax.ppermute(value, ("z", "core"), pairs)

    def add(*terms):
        return sum(term.astype(F32) for term in terms).astype(BF16)

    side = model // 2

    def total(here_left, here_right, down_left, up_right, up_left, down_right):
        left, right = add(here_left, down_left, up_left), add(here_right, up_right, down_right)
        return jnp.concatenate([left, right], axis=1)

    ring = hop(mine, 1, 0), hop(theirs, -1, 1)
    swapped = hop(theirs, 0, 1)
    *near, w_value_other, w_out_other = project(weights[:4], (mine, swapped), (weights[3], weights[5]))
    weights = (*weights[:3], w_value_other, weights[4], w_out_other)
    near, mine, theirs, crossing = lax.optimization_barrier((near, mine, theirs, crossing))
    ring_after = hop(theirs, 1, 1), hop(mine, -1, 0)
    crossing = lax.ppermute(crossing, ("seq", "core"), [(2 * i + 2, 2 * i + 1) for i in range(n_seq - 1)])
    half_rows = mine.shape[0] // 2
    far_a = hop(ring[0][:half_rows], 1, 0), hop(ring[1][:half_rows], -1, 0)
    near = (*near, *project(weights[:4], ring), *project(weights[:4], ring_after))
    far_a, near, later = lax.optimization_barrier((far_a, near, (ring[0][half_rows:], ring[1][half_rows:])))
    far_b = hop(later[0], 1, 0), hop(later[1], -1, 0)

    sums_a = attend(0, places_a, second_queries, crossing, near, far_a, weights)
    sums_a, far_b = lax.optimization_barrier((sums_a, far_b))
    up_a, down_a, above_a, below_a, *here_a = sums_a
    up_a, down_a = step(up_a, "z", 1), step(down_a, "z", -1)
    sums_b = attend(1, places_b, first_queries, crossing, near, far_b, weights)
    up_a, down_a, sums_b = lax.optimization_barrier((up_a, down_a, sums_b))
    above_a, below_a = lax.optimization_barrier((add(above_a, up_a[:, :side]), add(below_a, down_a[:, side:])))
    up_left_a, down_right_a = step(above_a, "z", 1), step(below_a, "z", -1)
    up_b, down_b = step(sums_b[0], "z", 1), step(sums_b[1], "z", -1)
    up_right_b, down_left_b = step(sums_b[3], "z", 1), step(sums_b[4], "z", -1)
    out_a = total(*here_a, down_a[:, :side], up_a[:, side:], up_left_a, down_right_a)

    pairs = []
    for i in range(0, n_seq * N_Z * N_CORE, 2):
        pairs.append((i, i + 1))
        if i % (N_Z * N_CORE):
            pairs.append((i + 1, i))
        elif i + N_Z * N_CORE < n_seq * N_Z * N_CORE:
            pairs.append((i + 1, i + N_Z * N_CORE))
    head = lax.ppermute(out_a, ("seq", "z", "core"), pairs)
    above_b, below_b = lax.optimization_barrier((add(sums_b[2], up_b), add(sums_b[5], down_b)))
    up_left_b, down_right_b = step(above_b, "z", 1), step(below_b, "z", -1)
    out_b = total(*sums_b[6:], down_left_b, up_right_b, up_left_b, down_right_b)
    return jnp.concatenate([head[1:], out_b, out_a[:1]], axis=0)


def solution(mesh):
    n_seq = mesh.devices.shape[0]
    fine = Mesh(mesh.devices.reshape(n_seq, N_Z, N_CORE), ("seq", "z", "core"))
    db = ("z", "core")
    return jax.shard_map(
        body,
        mesh=fine,
        in_specs=(
            P("seq", None),
            P(None, db),
            P(None, db),
            P(None, db),
            P(db, None),
            P("seq", None, None),
            P(),
            P(),
        ),
        out_specs=P(("seq", "z", "core"), None),
        check_vma=False,
    )
```

```python
import functools
import math

import jax
import jax.numpy as jnp
from jax import lax
from jax.experimental import pallas as pl
from jax.experimental.pallas import tpu as pltpu
from jax.sharding import Mesh, PartitionSpec as P

HS = 128
CL = 64
NB_LEN = 128
NEIGH = 2
N_Z = 4
N_CORE = 2
BLOCK = 128
F32 = jnp.float32
BF16 = jnp.bfloat16
SHARE = 0.4
LIMIT = 60 * 1024 * 1024
GRANT = 32 * 1024 * 1024


def step(value, axis, steps):
    count = lax.axis_size(axis)
    return lax.ppermute(value, axis, [(i, (i + steps) % count) for i in range(count)])


def cost(flops):
    return pl.CostEstimate(flops=int(flops * SHARE), bytes_accessed=int(flops * SHARE / 1000), transcendentals=0)


def dot(a, b):
    return jnp.dot(a, b, preferred_element_type=F32)


def bucket_places(shards):
    count = shards.shape[1]
    same_shard = shards[:, :, None] == shards[:, None, :]
    earlier = jnp.arange(count)[None, :] < jnp.arange(count)[:, None]
    return jnp.sum((same_shard & earlier[None]).astype(jnp.int32), axis=2)


def pick_kernel(index_ref, start_ref, source_ref, *refs):
    out_refs, rows_ref, sem = refs[:-2], refs[-2], refs[-1]
    rows = rows_ref.shape[1]
    start = pl.multiple_of(start_ref[0] * rows, rows)
    copy = pltpu.make_async_copy(source_ref.at[:, pl.ds(start, rows)], rows_ref, sem)
    copy.start()
    copy.wait()
    place = 0
    for out_ref in out_refs:
        for i in range(out_ref.shape[0]):
            out_ref[i] = rows_ref[index_ref[place]]
            place += 1


def pick(source, index, start, rows, counts, limit):
    shapes = [(count, rows, source.shape[2]) for count in counts]
    return pl.pallas_call(
        pick_kernel,
        grid_spec=pltpu.PrefetchScalarGridSpec(
            num_scalar_prefetch=2,
            grid=(1,),
            in_specs=[pl.BlockSpec(memory_space=pltpu.HBM)],
            out_specs=[pl.BlockSpec(shape, lambda i, index, start: (0, 0, 0)) for shape in shapes],
            scratch_shapes=[pltpu.VMEM((source.shape[0], rows, source.shape[2]), source.dtype), pltpu.SemaphoreType.DMA],
        ),
        out_shape=[jax.ShapeDtypeStruct(shape, source.dtype) for shape in shapes],
        cost_estimate=cost(1e9),
        compiler_params=pltpu.CompilerParams(vmem_limit_bytes=limit * 1024 * 1024),
    )(index, start.reshape(1), source)


def query_kernel(core_ref, x_hbm, wa_hbm, wb_hbm, first_ref, second_ref, crossing_ref, x_ref, wa_ref, wb_ref, sems):
    half = wa_ref.shape[1]
    copies = []
    for j in range(N_Z):
        block = N_CORE * j + core_ref[0]
        after = lax.rem(block + 1, N_Z * N_CORE)
        copies.append(pltpu.make_async_copy(x_hbm.at[block], x_ref.at[j, :BLOCK], sems.at[2 * j]))
        copies.append(pltpu.make_async_copy(x_hbm.at[after, :CL], x_ref.at[j, BLOCK:], sems.at[2 * j + 1]))
    copies.append(pltpu.make_async_copy(wa_hbm, wa_ref, sems.at[2 * N_Z]))
    copies.append(pltpu.make_async_copy(wb_hbm, wb_ref, sems.at[2 * N_Z + 1]))
    for copy in copies:
        copy.start()
    for j in range(N_Z):
        copies[2 * j].wait()
        copies[2 * j + 1].wait()
        source = x_ref[j].astype(F32)
        scale = lax.rsqrt(jnp.mean(source * source, axis=-1, keepdims=True) + 1e-05)
        x_ref[j] = (source * scale).astype(BF16)
    rows = BLOCK + CL
    for i, weight_ref in enumerate((wa_ref, wb_ref)):
        copies[2 * N_Z + i].wait()
        here, there = slice(i * half, (i + 1) * half), slice((1 - i) * half, (2 - i) * half)
        product = dot(x_ref[...].reshape(N_Z * rows, -1), weight_ref[...])
        for j in range(N_Z):
            rolled = pltpu.roll(product[j * rows : (j + 1) * rows], 1, 0).astype(BF16)
            first_ref[j, :, here] = rolled[CL:BLOCK]
            second_ref[j, :, here] = rolled[BLOCK:]
            if j == 0:
                crossing_ref[:, there] = rolled[:CL]


def project_queries(decoder, weight_a, weight_b, core):
    model, half = weight_a.shape
    blocks = decoder.reshape(N_Z * N_CORE, BLOCK, model)
    shape = (N_Z, CL, 2 * half)
    out_spec = pl.BlockSpec(shape, lambda i, core: (0, 0, 0))
    return pl.pallas_call(
        query_kernel,
        grid_spec=pltpu.PrefetchScalarGridSpec(
            num_scalar_prefetch=1,
            grid=(1,),
            in_specs=[pl.BlockSpec(memory_space=pltpu.HBM)] * 3,
            out_specs=[out_spec, out_spec, pl.BlockSpec(shape[1:], lambda i, core: (0, 0))],
            scratch_shapes=[
                pltpu.VMEM((N_Z, BLOCK + CL, model), BF16),
                pltpu.VMEM((model, half), BF16),
                pltpu.VMEM((model, half), BF16),
                pltpu.SemaphoreType.DMA((2 * N_Z + 2,)),
            ],
        ),
        out_shape=[jax.ShapeDtypeStruct(dims, BF16) for dims in (shape, shape, shape[1:])],
        cost_estimate=cost(3e9),
        compiler_params=pltpu.CompilerParams(vmem_limit_bytes=LIMIT),
    )(core.reshape(1), blocks, weight_a, weight_b)


def project_kernel(count, *refs):
    low_ref, high_ref, weight_refs, carried_hbm = refs[0], refs[1], refs[2:6], refs[6 : 6 + count]
    out_refs, carried_refs = refs[6 + count : 10 + count], refs[10 + count : 10 + 2 * count]
    copies = [pltpu.make_async_copy(carried_hbm[i], carried_refs[i], refs[-1].at[i]) for i in range(count)]
    for copy in copies:
        copy.start()
    rows = jnp.concatenate([low_ref[...], high_ref[...]], axis=0)
    for weight_ref, out_ref in zip(weight_refs, out_refs):
        out_ref[...] = dot(rows, weight_ref[...]).astype(BF16).reshape(out_ref.shape)
    for copy in copies:
        copy.wait()


def project(weights, parts, carried=()):
    rows, enc = parts[0].shape
    width = weights[0].shape[1]
    shape = (len(parts), 2, N_Z, rows // (2 * N_Z), width)
    vmem = pl.BlockSpec(memory_space=pltpu.VMEM)
    return pl.pallas_call(
        functools.partial(project_kernel, len(carried)),
        in_specs=[vmem] * 6 + [pl.BlockSpec(memory_space=pltpu.HBM)] * len(carried),
        out_specs=[vmem] * (4 + len(carried)),
        out_shape=[jax.ShapeDtypeStruct(shape, BF16)] * 4
        + [jax.ShapeDtypeStruct(value.shape, value.dtype) for value in carried],
        scratch_shapes=[pltpu.SemaphoreType.DMA((max(1, len(carried)),))],
        cost_estimate=cost(2e9),
        compiler_params=pltpu.CompilerParams(vmem_limit_bytes=GRANT),
    )(*parts, *weights, *carried)


def span_kernel(group, place_ref, *refs):
    refs = list(refs)

    def take(count):
        taken = refs[:count]
        del refs[:count]
        return taken

    near_refs, row_refs, weight_refs = take(12), take(2), take(4)
    q_ref, crossing_ref = take(2)
    out_weight_refs, out_refs, far_kv_refs = take(2), take(6 if group == 0 else 8), take(4)
    rows = jnp.concatenate([ref[...] for ref in row_refs], axis=0)
    for weight_ref, far_kv_ref in zip(weight_refs, far_kv_refs):
        far_kv_ref[...] = dot(rows, weight_ref[...]).astype(BF16).reshape(far_kv_ref.shape)
    (context_ref,) = refs
    half, model = out_weight_refs[0].shape
    is_first_row = lax.broadcasted_iota(jnp.int32, (CL, HS), 0) == 0
    heads = [(side, lower) for side in (0, 1) for lower in range(0, half, HS)]

    def attend_span(span, carry):
        def columns(i, lower):
            parts = [near_refs[j][:, group, span, :, lower : lower + HS] for j in range(i, 12, 4)]
            parts.append(far_kv_refs[i][:, span, :, lower : lower + HS])
            return jnp.concatenate([part.reshape(-1, HS) for part in parts], axis=0)

        crosses = (span == N_Z - 1) & (place_ref[N_Z] == 1)
        scores = []
        for side, lower in heads:
            place = slice(side * half + lower, side * half + lower + HS)
            q = q_ref[span, :, place]
            if group == 0:
                q = jnp.where(is_first_row | jnp.logical_not(crosses), q, crossing_ref[:, place])
            k = columns(2 * side, lower)
            scores.append(lax.dot_general(q, k, (((1,), (1,)), ((), ())), preferred_element_type=F32))
        probs = []
        for score in scores:
            score = score * (1.0 / math.sqrt(HS))
            weights = jnp.exp(score - jnp.max(score, axis=-1, keepdims=True))
            total = jnp.sum(weights, axis=-1, keepdims=True)
            probs.append((weights * (1.0 / total)).astype(BF16))
        for (side, lower), prob in zip(heads, probs):
            v = columns(2 * side + 1, lower)
            context_ref[span, :, side * half + lower : side * half + lower + HS] = dot(prob, v).astype(BF16)
        return carry

    lax.fori_loop(0, N_Z, attend_span, 0, unroll=N_Z)

    blocks = [context_ref[place_ref[i]] for i in range(N_Z)]
    if group == 0:
        is_first_row = lax.broadcasted_iota(jnp.int32, blocks[0].shape, 0) == 0
        blocks = [jnp.where(is_first_row, context_ref[place_ref[N_Z + 1 + i]], blocks[i]) for i in range(N_Z)]
    context = jnp.concatenate(blocks, axis=0)
    tile = model // 4
    for lower in range(0, model, tile):
        place = slice(lower, lower + tile)
        product = dot(context[:, :half], out_weight_refs[0][:, place])
        product = (product + dot(context[:, half:], out_weight_refs[1][:, place])).astype(BF16)
        side, start = lower // (model // 2), lower % (model // 2)
        for i in range(N_Z):
            block = product[i * CL : (i + 1) * CL]
            if group == 1:
                out_refs[2 * i + side][:, start : start + tile] = block
            elif i < N_Z - 1 and (i, side) not in ((1, 0), (2, 1)):
                out_refs[(0, 0, 1)[i] if i != 0 else side][:, place] = block
            else:
                out_refs[{(1, 0): 2, (2, 1): 3, (3, 0): 4, (3, 1): 5}[i, side]][:, start : start + tile] = block


def attend(group, places, queries, crossing, near, far, weights):
    spans, tokens, width = queries.shape
    half, model = weights[4].shape
    outs = [(tokens, model)] * 2 + [(tokens, model // 2)] * 4 if group == 0 else [(tokens, model // 2)] * 8
    scratch = [(2, spans, near[0].shape[3], half)] * 4 + [queries.shape]
    operands = (*near, *far, *weights[:4], queries, crossing, *weights[4:])
    vmem = pl.BlockSpec(memory_space=pltpu.VMEM)
    return pl.pallas_call(
        functools.partial(span_kernel, group),
        grid_spec=pltpu.PrefetchScalarGridSpec(
            num_scalar_prefetch=1,
            grid=(),
            in_specs=[vmem] * len(operands),
            out_specs=[vmem] * len(outs),
            scratch_shapes=[pltpu.VMEM(shape, BF16) for shape in scratch],
        ),
        out_shape=[jax.ShapeDtypeStruct(shape, BF16) for shape in outs],
        cost_estimate=cost(5e9),
        compiler_params=pltpu.CompilerParams(vmem_limit_bytes=GRANT),
    )(places, *operands)


def assemble_kernel(head_ref, first_ref, *refs):
    out_ref, side = refs[-1], refs[0].shape[1]
    rows = lax.broadcasted_iota(jnp.int32, (BLOCK, side), 0)
    for i in range(2):
        place = slice(i * side, (i + 1) * side)
        total = refs[i][...].astype(F32) + refs[2 + i][...].astype(F32) + refs[4 + i][...].astype(F32)
        both = jnp.concatenate([head_ref[:, place].astype(F32), total], axis=0)
        rolled = pltpu.roll(both, BLOCK - 1, 0)
        out_ref[:, place] = jnp.where(rows == BLOCK - 1, first_ref[:1, place].astype(F32), rolled).astype(BF16)


def assemble(head, first, here, direct, summed):
    vmem = pl.BlockSpec(memory_space=pltpu.VMEM)
    return pl.pallas_call(
        assemble_kernel,
        in_specs=[vmem] * 8,
        out_specs=vmem,
        out_shape=jax.ShapeDtypeStruct((BLOCK, head.shape[1]), BF16),
        cost_estimate=cost(1e8),
        compiler_params=pltpu.CompilerParams(vmem_limit_bytes=24 * 1024 * 1024),
    )(head, first, *here, *direct, *summed)


def body(decoder, w_query, w_key, w_value, w_out, database, nb_shard, nb_slot):
    n_seq = lax.axis_size("seq")
    seq_index, z_index, core = lax.axis_index("seq"), lax.axis_index("z"), lax.axis_index("core")
    tok_rows, model = decoder.shape
    spans = tok_rows // CL
    requests = NEIGH * spans
    capacity = (requests + n_seq - 1) // n_seq + 1
    slots, _, enc = database.shape
    piece = NB_LEN // (N_Z * N_CORE)

    bits = (slots - 1).bit_length()
    lists = (nb_shard.T << bits) + nb_slot.T
    lists = lists.reshape(NEIGH, n_seq, spans).transpose(1, 0, 2).reshape(n_seq, requests)
    shard_lists, slot_lists = lists >> bits, lists & ((1 << bits) - 1)
    places = bucket_places(shard_lists)
    picked = (shard_lists == seq_index)[:, None, :] & (places[:, None, :] == jnp.arange(capacity)[None, :, None])
    send_slot = jnp.sum(jnp.where(picked, slot_lists[:, None, :], 0), axis=2)
    (outgoing,) = pick(database, send_slot.reshape(-1), z_index * N_CORE + core, piece, [n_seq * capacity], 60)
    received = lax.all_to_all(
        outgoing.reshape(n_seq, capacity, piece, enc), "seq", split_axis=0, concat_axis=0, tiled=True
    )
    received = received.reshape(n_seq * capacity, piece, enc)

    w_query_other = step(w_query, "core", 1)
    weights = (w_key, w_value, *(step(weight, "core", 1) for weight in (w_key, w_value)), w_out, step(w_out, "core", 1))
    first_queries, second_queries, crossing = project_queries(decoder, w_query, w_query_other, core)
    distance = jnp.array([2, 1, 3, 0], jnp.int32)
    places_b = (z_index + distance) % N_Z
    places_a = (z_index + distance + (N_Z - 1) * core) % N_Z
    places_a = jnp.concatenate([places_a, core.reshape(1), places_b]).astype(jnp.int32)
    received, weights, crossing, places_a, places_b = lax.optimization_barrier(
        (received, weights, crossing, places_a, places_b)
    )

    my_shards = lax.dynamic_index_in_dim(shard_lists, seq_index, 0, keepdims=False)
    my_places = lax.dynamic_index_in_dim(places, seq_index, 0, keepdims=False)
    row_index = (my_shards * capacity + my_places).reshape(NEIGH, N_Z, N_CORE, 2)
    row_index = row_index.transpose(2, 3, 1, 0)[:, ::-1]
    row_index = jnp.where(core == 0, row_index, row_index[::-1]).reshape(-1)
    count = row_index.shape[0] // 2
    mine, theirs = pick(received, row_index, jnp.zeros((), jnp.int32), piece, [count] * 2, 30)
    mine, theirs = mine.reshape(-1, enc), theirs.reshape(-1, enc)

    def hop(value, steps, cross):
        pairs = [
            (z * N_CORE + c, (z + steps) % N_Z * N_CORE + (c + cross) % N_CORE)
            for z in range(N_Z)
            for c in range(N_CORE)
        ]
        return lax.ppermute(value, ("z", "core"), pairs)

    def add(*terms):
        return sum(term.astype(F32) for term in terms).astype(BF16)

    side = model // 2

    def total(here_left, here_right, down_left, up_right, up_left, down_right):
        left, right = add(here_left, down_left, up_left), add(here_right, up_right, down_right)
        return jnp.concatenate([left, right], axis=1)

    ring = hop(mine, 1, 0), hop(theirs, -1, 1)
    swapped = hop(theirs, 0, 1)
    *near, w_value_other, w_out_other = project(weights[:4], (mine, swapped), (weights[3], weights[5]))
    weights = (*weights[:3], w_value_other, weights[4], w_out_other)
    near, mine, theirs, crossing = lax.optimization_barrier((near, mine, theirs, crossing))
    ring_after = hop(theirs, 1, 1), hop(mine, -1, 0)
    crossing = lax.ppermute(crossing, ("seq", "core"), [(2 * i + 2, 2 * i + 1) for i in range(n_seq - 1)])
    half_rows = mine.shape[0] // 2
    far_a = hop(ring[0][:half_rows], 1, 0), hop(ring[1][:half_rows], -1, 0)
    near = (*near, *project(weights[:4], ring), *project(weights[:4], ring_after))
    far_a, near, later = lax.optimization_barrier((far_a, near, (ring[0][half_rows:], ring[1][half_rows:])))
    far_b = hop(later[0], 1, 0), hop(later[1], -1, 0)

    sums_a = attend(0, places_a, second_queries, crossing, near, far_a, weights)
    sums_a, far_b = lax.optimization_barrier((sums_a, far_b))
    up_a, down_a, above_a, below_a, *here_a = sums_a
    up_a, down_a = step(up_a, "z", 1), step(down_a, "z", -1)
    sums_b = attend(1, places_b, first_queries, crossing, near, far_b, weights)
    up_a, down_a, sums_b = lax.optimization_barrier((up_a, down_a, sums_b))
    above_a, below_a = lax.optimization_barrier((add(above_a, up_a[:, :side]), add(below_a, down_a[:, side:])))
    up_left_a, down_right_a = step(above_a, "z", 1), step(below_a, "z", -1)
    up_b, down_b = step(sums_b[0], "z", 1), step(sums_b[1], "z", -1)
    up_right_b, down_left_b = step(sums_b[3], "z", 1), step(sums_b[4], "z", -1)
    out_a = total(*here_a, down_a[:, :side], up_a[:, side:], up_left_a, down_right_a)

    pairs = []
    for i in range(0, n_seq * N_Z * N_CORE, 2):
        pairs.append((i, i + 1))
        if i % (N_Z * N_CORE):
            pairs.append((i + 1, i))
        elif i + N_Z * N_CORE < n_seq * N_Z * N_CORE:
            pairs.append((i + 1, i + N_Z * N_CORE))
    head = lax.ppermute(out_a, ("seq", "z", "core"), pairs)
    above_b, below_b = lax.optimization_barrier((add(sums_b[2], up_b), add(sums_b[5], down_b)))
    up_left_b, down_right_b = step(above_b, "z", 1), step(below_b, "z", -1)
    return assemble(head, out_a, sums_b[6:], (down_left_b, up_right_b), (up_left_b, down_right_b))


def solution(mesh):
    n_seq = mesh.devices.shape[0]
    fine = Mesh(mesh.devices.reshape(n_seq, N_Z, N_CORE), ("seq", "z", "core"))
    db = ("z", "core")
    return jax.shard_map(
        body,
        mesh=fine,
        in_specs=(
            P("seq", None),
            P(None, db),
            P(None, db),
            P(None, db),
            P(db, None),
            P("seq", None, None),
            P(),
            P(),
        ),
        out_specs=P(("seq", "z", "core"), None),
        check_vma=False,
    )
```

```python
import functools
import math

import jax
import jax.numpy as jnp
from jax import lax
from jax.experimental import pallas as pl
from jax.experimental.pallas import tpu as pltpu
from jax.sharding import Mesh, PartitionSpec as P

HS = 128
CL = 64
NB_LEN = 128
NEIGH = 2
N_Z = 4
N_CORE = 2
BLOCK = 128
F32 = jnp.float32
BF16 = jnp.bfloat16
SHARE = 0.4
LIMIT = 60 * 1024 * 1024
GRANT = 26 * 1024 * 1024


def step(value, axis, steps):
    count = lax.axis_size(axis)
    return lax.ppermute(value, axis, [(i, (i + steps) % count) for i in range(count)])


def cost(flops):
    return pl.CostEstimate(flops=int(flops * SHARE), bytes_accessed=int(flops * SHARE / 1000), transcendentals=0)


def dot(a, b):
    return jnp.dot(a, b, preferred_element_type=F32)


def bucket_places(shards):
    count = shards.shape[1]
    same_shard = shards[:, :, None] == shards[:, None, :]
    earlier = jnp.arange(count)[None, :] < jnp.arange(count)[:, None]
    return jnp.sum((same_shard & earlier[None]).astype(jnp.int32), axis=2)


def pick_kernel(index_ref, start_ref, source_ref, *refs):
    out_refs, rows_ref, sem = refs[:-2], refs[-2], refs[-1]
    rows = rows_ref.shape[1]
    start = pl.multiple_of(start_ref[0] * rows, rows)
    copy = pltpu.make_async_copy(source_ref.at[:, pl.ds(start, rows)], rows_ref, sem)
    copy.start()
    copy.wait()
    place = 0
    for out_ref in out_refs:
        for i in range(out_ref.shape[0]):
            out_ref[i] = rows_ref[index_ref[place]]
            place += 1


def pick(source, index, start, rows, counts, limit):
    shapes = [(count, rows, source.shape[2]) for count in counts]
    return pl.pallas_call(
        pick_kernel,
        grid_spec=pltpu.PrefetchScalarGridSpec(
            num_scalar_prefetch=2,
            grid=(1,),
            in_specs=[pl.BlockSpec(memory_space=pltpu.HBM)],
            out_specs=[pl.BlockSpec(shape, lambda i, index, start: (0, 0, 0)) for shape in shapes],
            scratch_shapes=[pltpu.VMEM((source.shape[0], rows, source.shape[2]), source.dtype), pltpu.SemaphoreType.DMA],
        ),
        out_shape=[jax.ShapeDtypeStruct(shape, source.dtype) for shape in shapes],
        cost_estimate=cost(1e9),
        compiler_params=pltpu.CompilerParams(vmem_limit_bytes=limit * 1024 * 1024),
    )(index, start.reshape(1), source)


def query_kernel(core_ref, x_hbm, wa_hbm, wb_hbm, first_ref, second_ref, crossing_ref, x_ref, wa_ref, wb_ref, sems):
    half = wa_ref.shape[1]
    copies = []
    for j in range(N_Z):
        block = N_CORE * j + core_ref[0]
        after = lax.rem(block + 1, N_Z * N_CORE)
        copies.append(pltpu.make_async_copy(x_hbm.at[block], x_ref.at[j, :BLOCK], sems.at[2 * j]))
        copies.append(pltpu.make_async_copy(x_hbm.at[after, :CL], x_ref.at[j, BLOCK:], sems.at[2 * j + 1]))
    copies.append(pltpu.make_async_copy(wa_hbm, wa_ref, sems.at[2 * N_Z]))
    copies.append(pltpu.make_async_copy(wb_hbm, wb_ref, sems.at[2 * N_Z + 1]))
    for copy in copies:
        copy.start()
    for j in range(N_Z):
        copies[2 * j].wait()
        copies[2 * j + 1].wait()
        source = x_ref[j].astype(F32)
        scale = lax.rsqrt(jnp.mean(source * source, axis=-1, keepdims=True) + 1e-05)
        x_ref[j] = (source * scale).astype(BF16)
    rows = BLOCK + CL
    for i, weight_ref in enumerate((wa_ref, wb_ref)):
        copies[2 * N_Z + i].wait()
        here, there = slice(i * half, (i + 1) * half), slice((1 - i) * half, (2 - i) * half)
        product = dot(x_ref[...].reshape(N_Z * rows, -1), weight_ref[...])
        for j in range(N_Z):
            rolled = pltpu.roll(product[j * rows : (j + 1) * rows], 1, 0).astype(BF16)
            first_ref[j, :, here] = rolled[CL:BLOCK]
            second_ref[j, :, here] = rolled[BLOCK:]
            if j == 0:
                crossing_ref[:, there] = rolled[:CL]


def project_queries(decoder, weight_a, weight_b, core):
    model, half = weight_a.shape
    blocks = decoder.reshape(N_Z * N_CORE, BLOCK, model)
    shape = (N_Z, CL, 2 * half)
    out_spec = pl.BlockSpec(shape, lambda i, core: (0, 0, 0))
    return pl.pallas_call(
        query_kernel,
        grid_spec=pltpu.PrefetchScalarGridSpec(
            num_scalar_prefetch=1,
            grid=(1,),
            in_specs=[pl.BlockSpec(memory_space=pltpu.HBM)] * 3,
            out_specs=[out_spec, out_spec, pl.BlockSpec(shape[1:], lambda i, core: (0, 0))],
            scratch_shapes=[
                pltpu.VMEM((N_Z, BLOCK + CL, model), BF16),
                pltpu.VMEM((model, half), BF16),
                pltpu.VMEM((model, half), BF16),
                pltpu.SemaphoreType.DMA((2 * N_Z + 2,)),
            ],
        ),
        out_shape=[jax.ShapeDtypeStruct(dims, BF16) for dims in (shape, shape, shape[1:])],
        cost_estimate=cost(3e9),
        compiler_params=pltpu.CompilerParams(vmem_limit_bytes=LIMIT),
    )(core.reshape(1), blocks, weight_a, weight_b)


def project_kernel(count, *refs):
    low_ref, high_ref, weight_refs, carried_hbm = refs[0], refs[1], refs[2:6], refs[6 : 6 + count]
    out_refs, carried_refs = refs[6 + count : 10 + count], refs[10 + count : 10 + 2 * count]
    copies = [pltpu.make_async_copy(carried_hbm[i], carried_refs[i], refs[-1].at[i]) for i in range(count)]
    for copy in copies:
        copy.start()
    rows = jnp.concatenate([low_ref[...], high_ref[...]], axis=0)
    for weight_ref, out_ref in zip(weight_refs, out_refs):
        out_ref[...] = dot(rows, weight_ref[...]).astype(BF16).reshape(out_ref.shape)
    for copy in copies:
        copy.wait()


def project(weights, parts, carried=()):
    rows, enc = parts[0].shape
    width = weights[0].shape[1]
    shape = (len(parts), 2, N_Z, rows // (2 * N_Z), width)
    vmem = pl.BlockSpec(memory_space=pltpu.VMEM)
    return pl.pallas_call(
        functools.partial(project_kernel, len(carried)),
        in_specs=[vmem] * 6 + [pl.BlockSpec(memory_space=pltpu.HBM)] * len(carried),
        out_specs=[vmem] * (4 + len(carried)),
        out_shape=[jax.ShapeDtypeStruct(shape, BF16)] * 4
        + [jax.ShapeDtypeStruct(value.shape, value.dtype) for value in carried],
        scratch_shapes=[pltpu.SemaphoreType.DMA((max(1, len(carried)),))],
        cost_estimate=cost(2e9),
        compiler_params=pltpu.CompilerParams(vmem_limit_bytes=18 * 1024 * 1024),
    )(*parts, *weights, *carried)


def span_kernel(group, place_ref, *refs):
    refs = list(refs)

    def take(count):
        taken = refs[:count]
        del refs[:count]
        return taken

    near_refs, row_refs, weight_refs = take(12), take(2), take(4)
    q_ref, crossing_ref = take(2)
    out_weight_refs, out_refs, far_kv_refs = take(2), take(6 if group == 0 else 8), take(4)
    rows = jnp.concatenate([ref[...] for ref in row_refs], axis=0)
    for weight_ref, far_kv_ref in zip(weight_refs, far_kv_refs):
        far_kv_ref[...] = dot(rows, weight_ref[...]).astype(BF16).reshape(far_kv_ref.shape)
    (context_ref,) = refs
    half, model = out_weight_refs[0].shape
    is_first_row = lax.broadcasted_iota(jnp.int32, (CL, HS), 0) == 0
    heads = [(side, lower) for side in (0, 1) for lower in range(0, half, HS)]

    def attend_span(span, carry):
        def columns(i, lower):
            parts = [near_refs[j][:, group, span, :, lower : lower + HS] for j in range(i, 12, 4)]
            parts.append(far_kv_refs[i][:, span, :, lower : lower + HS])
            return jnp.concatenate([part.reshape(-1, HS) for part in parts], axis=0)

        crosses = (span == N_Z - 1) & (place_ref[N_Z] == 1)
        scores = []
        for side, lower in heads:
            place = slice(side * half + lower, side * half + lower + HS)
            q = q_ref[span, :, place]
            if group == 0:
                q = jnp.where(is_first_row | jnp.logical_not(crosses), q, crossing_ref[:, place])
            k = columns(2 * side, lower)
            scores.append(lax.dot_general(q, k, (((1,), (1,)), ((), ())), preferred_element_type=F32))
        probs = []
        for score in scores:
            score = score * (1.0 / math.sqrt(HS))
            weights = jnp.exp(score - jnp.max(score, axis=-1, keepdims=True))
            total = jnp.sum(weights, axis=-1, keepdims=True)
            probs.append((weights * (1.0 / total)).astype(BF16))
        for (side, lower), prob in zip(heads, probs):
            v = columns(2 * side + 1, lower)
            context_ref[span, :, side * half + lower : side * half + lower + HS] = dot(prob, v).astype(BF16)
        return carry

    lax.fori_loop(0, N_Z, attend_span, 0, unroll=N_Z)

    blocks = [context_ref[place_ref[i]] for i in range(N_Z)]
    if group == 0:
        is_first_row = lax.broadcasted_iota(jnp.int32, blocks[0].shape, 0) == 0
        blocks = [jnp.where(is_first_row, context_ref[place_ref[N_Z + 1 + i]], blocks[i]) for i in range(N_Z)]
    context = jnp.concatenate(blocks, axis=0)
    tile = model // 4
    for lower in range(0, model, tile):
        place = slice(lower, lower + tile)
        product = dot(context[:, :half], out_weight_refs[0][:, place])
        product = (product + dot(context[:, half:], out_weight_refs[1][:, place])).astype(BF16)
        side, start = lower // (model // 2), lower % (model // 2)
        for i in range(N_Z):
            block = product[i * CL : (i + 1) * CL]
            if group == 1:
                out_refs[2 * i + side][:, start : start + tile] = block
            elif i < N_Z - 1 and (i, side) not in ((1, 0), (2, 1)):
                out_refs[(0, 0, 1)[i] if i != 0 else side][:, place] = block
            else:
                out_refs[{(1, 0): 2, (2, 1): 3, (3, 0): 4, (3, 1): 5}[i, side]][:, start : start + tile] = block


def attend(group, places, queries, crossing, near, far, weights):
    spans, tokens, width = queries.shape
    half, model = weights[4].shape
    outs = [(tokens, model)] * 2 + [(tokens, model // 2)] * 4 if group == 0 else [(tokens, model // 2)] * 8
    scratch = [(2, spans, near[0].shape[3], half)] * 4 + [queries.shape]
    operands = (*near, *far, *weights[:4], queries, crossing, *weights[4:])
    vmem = pl.BlockSpec(memory_space=pltpu.VMEM)
    return pl.pallas_call(
        functools.partial(span_kernel, group),
        grid_spec=pltpu.PrefetchScalarGridSpec(
            num_scalar_prefetch=1,
            grid=(),
            in_specs=[vmem] * len(operands),
            out_specs=[vmem] * len(outs),
            scratch_shapes=[pltpu.VMEM(shape, BF16) for shape in scratch],
        ),
        out_shape=[jax.ShapeDtypeStruct(shape, BF16) for shape in outs],
        cost_estimate=cost(5e9),
        compiler_params=pltpu.CompilerParams(vmem_limit_bytes=GRANT),
    )(places, *operands)


def body(decoder, w_query, w_key, w_value, w_out, database, nb_shard, nb_slot):
    n_seq = lax.axis_size("seq")
    seq_index, z_index, core = lax.axis_index("seq"), lax.axis_index("z"), lax.axis_index("core")
    tok_rows, model = decoder.shape
    spans = tok_rows // CL
    requests = NEIGH * spans
    capacity = (requests + n_seq - 1) // n_seq + 1
    slots, _, enc = database.shape
    piece = NB_LEN // (N_Z * N_CORE)

    bits = (slots - 1).bit_length()
    lists = (nb_shard.T << bits) + nb_slot.T
    lists = lists.reshape(NEIGH, n_seq, spans).transpose(1, 0, 2).reshape(n_seq, requests)
    shard_lists, slot_lists = lists >> bits, lists & ((1 << bits) - 1)
    places = bucket_places(shard_lists)
    picked = (shard_lists == seq_index)[:, None, :] & (places[:, None, :] == jnp.arange(capacity)[None, :, None])
    send_slot = jnp.sum(jnp.where(picked, slot_lists[:, None, :], 0), axis=2)
    (outgoing,) = pick(database, send_slot.reshape(-1), z_index * N_CORE + core, piece, [n_seq * capacity], 60)
    received = lax.all_to_all(
        outgoing.reshape(n_seq, capacity, piece, enc), "seq", split_axis=0, concat_axis=0, tiled=True
    )
    received = received.reshape(n_seq * capacity, piece, enc)

    w_query_other = step(w_query, "core", 1)
    weights = (w_key, w_value, *(step(weight, "core", 1) for weight in (w_key, w_value)), w_out, step(w_out, "core", 1))
    first_queries, second_queries, crossing = project_queries(decoder, w_query, w_query_other, core)
    distance = jnp.array([2, 1, 3, 0], jnp.int32)
    places_b = (z_index + distance) % N_Z
    places_a = (z_index + distance + (N_Z - 1) * core) % N_Z
    places_a = jnp.concatenate([places_a, core.reshape(1), places_b]).astype(jnp.int32)
    received, weights, crossing, places_a, places_b = lax.optimization_barrier(
        (received, weights, crossing, places_a, places_b)
    )

    my_shards = lax.dynamic_index_in_dim(shard_lists, seq_index, 0, keepdims=False)
    my_places = lax.dynamic_index_in_dim(places, seq_index, 0, keepdims=False)
    row_index = (my_shards * capacity + my_places).reshape(NEIGH, N_Z, N_CORE, 2)
    row_index = row_index.transpose(2, 3, 1, 0)[:, ::-1]
    row_index = jnp.where(core == 0, row_index, row_index[::-1]).reshape(-1)
    count = row_index.shape[0] // 2
    mine, theirs = pick(received, row_index, jnp.zeros((), jnp.int32), piece, [count] * 2, 10)
    mine, theirs = mine.reshape(-1, enc), theirs.reshape(-1, enc)

    def hop(value, steps, cross):
        pairs = [
            (z * N_CORE + c, (z + steps) % N_Z * N_CORE + (c + cross) % N_CORE)
            for z in range(N_Z)
            for c in range(N_CORE)
        ]
        return lax.ppermute(value, ("z", "core"), pairs)

    def add(*terms):
        return sum(term.astype(F32) for term in terms).astype(BF16)

    side = model // 2

    def total(here_left, here_right, down_left, up_right, up_left, down_right):
        left, right = add(here_left, down_left, up_left), add(here_right, up_right, down_right)
        return jnp.concatenate([left, right], axis=1)

    ring = hop(mine, 1, 0), hop(theirs, -1, 1)
    swapped = hop(theirs, 0, 1)
    *near, w_value_other, w_out_other = project(weights[:4], (mine, swapped), (weights[3], weights[5]))
    weights = (*weights[:3], w_value_other, weights[4], w_out_other)
    near, mine, theirs, crossing = lax.optimization_barrier((near, mine, theirs, crossing))
    ring_after = hop(theirs, 1, 1), hop(mine, -1, 0)
    crossing = lax.ppermute(crossing, ("seq", "core"), [(2 * i + 2, 2 * i + 1) for i in range(n_seq - 1)])
    half_rows = mine.shape[0] // 2
    far_a = hop(ring[0][:half_rows], 1, 0), hop(ring[1][:half_rows], -1, 0)
    near = (*near, *project(weights[:4], ring), *project(weights[:4], ring_after))
    far_a, near, later = lax.optimization_barrier((far_a, near, (ring[0][half_rows:], ring[1][half_rows:])))
    far_b = hop(later[0], 1, 0), hop(later[1], -1, 0)

    sums_a = attend(0, places_a, second_queries, crossing, near, far_a, weights)
    sums_a, far_b = lax.optimization_barrier((sums_a, far_b))
    up_a, down_a, above_a, below_a, *here_a = sums_a
    up_a, down_a = step(up_a, "z", 1), step(down_a, "z", -1)
    sums_b = attend(1, places_b, first_queries, crossing, near, far_b, weights)
    up_a, down_a, sums_b = lax.optimization_barrier((up_a, down_a, sums_b))
    above_a, below_a = lax.optimization_barrier((add(above_a, up_a[:, :side]), add(below_a, down_a[:, side:])))
    up_left_a, down_right_a = step(above_a, "z", 1), step(below_a, "z", -1)
    up_b, down_b = step(sums_b[0], "z", 1), step(sums_b[1], "z", -1)
    up_right_b, down_left_b = step(sums_b[3], "z", 1), step(sums_b[4], "z", -1)
    out_a = total(*here_a, down_a[:, :side], up_a[:, side:], up_left_a, down_right_a)

    pairs = []
    for i in range(0, n_seq * N_Z * N_CORE, 2):
        pairs.append((i, i + 1))
        if i % (N_Z * N_CORE):
            pairs.append((i + 1, i))
        elif i + N_Z * N_CORE < n_seq * N_Z * N_CORE:
            pairs.append((i + 1, i + N_Z * N_CORE))
    head = lax.ppermute(out_a, ("seq", "z", "core"), pairs)
    above_b, below_b = lax.optimization_barrier((add(sums_b[2], up_b), add(sums_b[5], down_b)))
    up_left_b, down_right_b = step(above_b, "z", 1), step(below_b, "z", -1)
    out_b = total(*sums_b[6:], down_left_b, up_right_b, up_left_b, down_right_b)
    return jnp.concatenate([head[1:], out_b, out_a[:1]], axis=0)


def solution(mesh):
    n_seq = mesh.devices.shape[0]
    fine = Mesh(mesh.devices.reshape(n_seq, N_Z, N_CORE), ("seq", "z", "core"))
    db = ("z", "core")
    return jax.shard_map(
        body,
        mesh=fine,
        in_specs=(
            P("seq", None),
            P(None, db),
            P(None, db),
            P(None, db),
            P(db, None),
            P("seq", None, None),
            P(),
            P(),
        ),
        out_specs=P(("seq", "z", "core"), None),
        check_vma=False,
    )
```
